512 devices in a mesh: pos: 64 (over z, x), tm: 8 (over y, core).
Axes of the slice: x: 4, y: 4, z: 16, core: 2. Of those that a mesh axis runs over, the one named last changes fastest.
Arguments:
- frames_in: bfloat16 [64, 512, 3072], P('pos'), may hold values from -24 to 24
- qkv_weight: bfloat16 [3072, 3, 3072], P('pos', None, 'tm'), may hold values from -0.109375 to 0.109375
- span_mask: int32 [8, 8], replicated, may hold values from 0 to 1, as said below
Outputs:
- attended: bfloat16 [64, 512, 3072], P('pos', None, 'tm')
The draws below stay inside these ranges and needn't reach their ends.
Inputs may be any that keep to these rules, and one draw needn't show every extreme that they name: span_mask has ones on the diagonal and zeros above it.
All inputs are finite; a program needn't handle non-finite values.
Results may differ from the reference program's by a relative error of at most 0.0078.
Values may be sent and summed in bfloat16 or wider, within the bound.
No kernel may reach another device: no remote copies, remote signals or barrier semaphores. Data moves between devices by JAX's collectives and lax.ppermute only.
A program may use at most 64 MiB of HBM per device.

```python
import jax
import jax.numpy as jnp
from jax import lax

D = 3072
HEADS = 24
HD = 128
FRAMES = 64
SPANS = 8
POS = 512


def draw_frames_in(key, part):
    key = jax.random.fold_in(key, 11)
    first = jax.random.fold_in(key, 0)
    values = jnp.clip(jax.random.normal(first, (FRAMES, POS, D), jnp.float32), -4.0, 4.0)
    return values.astype(jnp.bfloat16)


def draw_span_mask(key, part):
    key = jax.random.fold_in(key, 12)
    coins = jax.random.randint(key, (SPANS, SPANS), 0, 2, jnp.int32)
    below = jnp.tril(jnp.ones((SPANS, SPANS), jnp.int32), -1)
    return coins * below + jnp.eye(SPANS, dtype=jnp.int32)


def shard_levels(stream_key, dims, shards, smallest, high):
    gain = 1.0
    for axis_at, blocks in shards:
        draws = jax.random.uniform(jax.random.fold_in(jax.random.fold_in(stream_key, 6), axis_at), (blocks,), jnp.float32, smallest / len(shards), high / len(shards))
        gain = gain * jnp.repeat(jnp.exp(draws), dims[axis_at] // blocks).reshape((-1,) + (1,) * (len(dims) - 1 - axis_at))
    return gain


def gaussian(key, shape, width, bound, cuts=(), held_as=jnp.bfloat16):
    result = width * jax.random.normal(key, shape, jnp.float32)
    if cuts:
        result = result * shard_levels(key, shape, cuts, -0.22, 0.18)
    return jnp.clip(result, -bound, bound).astype(held_as)


def setup_inputs(seed: int = 0) -> dict:
    streams_of = jax.random.split(jax.random.key(seed), 4)
    frames_in = draw_frames_in(jax.random.fold_in(streams_of[3], 71), 0)
    qkv_weight = gaussian(streams_of[1], (D, 3, HEADS * HD), D ** -0.5, 0.109375, ((0, 64), (2, 8)))
    span_mask = draw_span_mask(jax.random.fold_in(streams_of[3], 71), 0)
    return dict(frames_in=frames_in, qkv_weight=qkv_weight, span_mask=span_mask)


def reference(frames_in, qkv_weight, span_mask):
    flat_weight = qkv_weight.reshape(D, 3 * HEADS * HD)

    def project(frame):
        return jnp.dot(frame, flat_weight, preferred_element_type=jnp.float32).astype(jnp.bfloat16)
    packed = lax.map(project, frames_in).reshape(FRAMES, POS, 3, HEADS, HD)
    query = packed[:, :, 0].astype(jnp.float32)
    keys = packed[:, :, 1].astype(jnp.float32)
    values = packed[:, :, 2].astype(jnp.float32)
    span_ids = (jnp.arange(FRAMES) // (FRAMES // SPANS)).astype(jnp.int32)
    allowed = span_mask[span_ids][:, span_ids] > 0
    scores = jnp.einsum('fphd,gphd->phfg', query, keys) * (1.0 / jnp.sqrt(jnp.float32(HD)))
    scores = jnp.where(allowed[None, None], scores, jnp.float32(-1e+30))
    row_max = lax.optimization_barrier(jnp.max(scores, axis=-1, keepdims=True))
    weights = jnp.where(allowed[None, None], jnp.exp(scores - row_max), jnp.float32(0.0))
    total = lax.optimization_barrier(jnp.sum(weights, axis=-1))
    rounded = weights.astype(jnp.bfloat16).astype(jnp.float32)
    summed = jnp.einsum('phfg,gphd->phfd', rounded, values) / total[..., None]
    attended = jnp.transpose(summed, (2, 0, 1, 3)).reshape(FRAMES, POS, HEADS * HD)
    return attended.astype(jnp.bfloat16)
```

```python
import jax
import jax.numpy as jnp
from jax import lax
from jax.experimental import pallas as pl
from jax.experimental.pallas import tpu as pltpu
from jax.sharding import Mesh
from jax.sharding import PartitionSpec as P

D = 3072
HD = 128
FRAMES = 64
SPANS = 8
GROUP = 384
NZ, NX, NY, NC = 16, 4, 4, 2
AXES = ("z", "x", "y", "c")
SLICE = D // (NZ * NX)
ROWS = NX * SLICE
TOKENS = FRAMES * 8


def permute(array, where_to):
    pairs = []
    for z in range(NZ):
        for x in range(NX):
            for y in range(NY):
                for c in range(NC):
                    a, b, d, e = where_to(z, x, y, c)
                    source = ((z * NX + x) * NY + y) * NC + c
                    pairs.append((source, (((a % NZ) * NX + b % NX) * NY + d % NY) * NC + e))
    return lax.ppermute(array, AXES, pairs)


def home(z, x, y, c):
    return (z, x, y, c) if c == x // 2 else (z, 3 - x, y, 1 - c)


def second(z, x, y, c):
    near = x ^ 1
    return (z, near if x // 2 == c else 3 - near, y, x // 2)


def swap(z, x, y, c):
    return (z, x, y, 1 - c)


def ring(z, x, y, c):
    return (z + (1 if c == 0 else -1), x, y, c)


def attend_kernel(place, mask, *refs):
    own, mine, theirs = refs[0], refs[1:9], refs[9:17]
    pieces = refs[17:21]
    out = refs[21]
    weights, tokens, qkv, bias, w_sems, x_sems = refs[22:]
    z, y, c = place[0], place[1], place[2]
    sign = 1 - 2 * c

    copies = []
    for i, (piece, shift) in enumerate(zip(pieces, (0, 1, 3, 2))):
        source = lax.rem(y + shift, NY)
        for half in range(2):
            at = pl.multiple_of((2 * source + half) * GROUP, GROUP)
            copies.append(
                pltpu.make_async_copy(piece.at[half], tokens.at[:, pl.ds(at, GROUP)], x_sems.at[2 * i + half])
            )
    by_part = []
    for j in range(3):
        part = []

        def add(ref, row):
            rows = ref.shape[1]
            at = pl.multiple_of(row, 32)
            part.append(
                pltpu.make_async_copy(ref.at[j], weights.at[j, pl.ds(at, rows)], w_sems.at[j, len(part)])
            )

        add(own, z * ROWS)
        for t in range(1, 8):
            add(mine[t - 1], lax.rem(z - sign * t + NZ, NZ) * ROWS)
            add(theirs[t - 1], lax.rem(z + sign * t + NZ, NZ) * ROWS)
        far = lax.rem(z + 8, NZ) * ROWS
        add(mine[7], far + c * (ROWS // 2))
        add(theirs[7], far + (1 - c) * (ROWS // 2))
        by_part.append(part)
    for copy in copies:
        copy.start()
    for part in by_part:
        for copy in part:
            copy.start()

    span_rows = TOKENS // SPANS
    column = lax.broadcasted_iota(jnp.int32, (1, TOKENS), 1)
    same = (
        lax.broadcasted_iota(jnp.int32, (span_rows, TOKENS), 0) & 7
    ) == (lax.broadcasted_iota(jnp.int32, (span_rows, TOKENS), 1) & 7)
    for i in range(SPANS):
        row = jnp.zeros((1, TOKENS), jnp.int32)
        for j in range(SPANS):
            row = jnp.where((column // span_rows) == j, mask[i, j], row)
        ok = same & (jnp.broadcast_to(row, (span_rows, TOKENS)) > 0)
        bias[pl.ds(i * span_rows, span_rows), :] = jnp.where(ok, 0.0, -1e30)

    for copy in copies:
        copy.wait()
    for j in range(3):
        for copy in by_part[j]:
            copy.wait()
        for r in range(2):
            rows = pl.ds(r * (TOKENS // 2), TOKENS // 2)
            qkv[j, rows, :] = jnp.dot(
                tokens[rows, :], weights[j], preferred_element_type=jnp.float32
            ).astype(jnp.bfloat16)

    scale = 1.0 / jnp.sqrt(jnp.float32(HD))
    for h in range(GROUP // HD):
        lanes = pl.ds(h * HD, HD)
        for i in range(4):
            rows = pl.ds(i * 128, 128)
            width = (i + 1) * 128
            scores = lax.dot_general(
                qkv[0, rows, lanes],
                qkv[1, pl.ds(0, width), lanes],
                (((1,), (1,)), ((), ())),
                preferred_element_type=jnp.float32,
            )
            scores = scores * scale + bias[rows, pl.ds(0, width)]
            shares = jnp.exp(scores - jnp.max(scores, axis=-1, keepdims=True))
            total = jnp.sum(shares, axis=-1, keepdims=True)
            summed = jnp.dot(
                shares.astype(jnp.bfloat16),
                qkv[2, pl.ds(0, width), lanes],
                preferred_element_type=jnp.float32,
            )
            out[rows, lanes] = (summed / total).astype(jnp.bfloat16)


def project_and_attend(place, span_mask, own, mine, theirs, pieces):
    arrays = [own, *mine, *theirs, *pieces]
    return pl.pallas_call(
        attend_kernel,
        out_shape=jax.ShapeDtypeStruct((TOKENS, GROUP), jnp.bfloat16),
        in_specs=[pl.BlockSpec(memory_space=pltpu.SMEM)] * 2
        + [pl.BlockSpec(memory_space=pl.ANY)] * len(arrays),
        out_specs=pl.BlockSpec(memory_space=pltpu.VMEM),
        scratch_shapes=[
            pltpu.VMEM((3, D, GROUP), jnp.bfloat16),
            pltpu.VMEM((TOKENS, D), jnp.bfloat16),
            pltpu.VMEM((3, TOKENS, GROUP), jnp.bfloat16),
            pltpu.VMEM((TOKENS, TOKENS), jnp.float32),
            pltpu.SemaphoreType.DMA((3, 17)),
            pltpu.SemaphoreType.DMA((8,)),
        ],
        compiler_params=pltpu.CompilerParams(vmem_limit_bytes=40 * 1024 * 1024),
    )(place, span_mask, *arrays)


def per_device(frames_in, qkv_weight, span_mask):
    z, x, y, c = (lax.axis_index(name) for name in AXES)
    group = x // 2

    piece = jnp.transpose(qkv_weight, (1, 0, 2))
    first = permute(piece, home)
    other = permute(piece, second)
    slot = jnp.where(c == group, x, 3 - x)
    half = jnp.where(
        slot % 2 == 0,
        jnp.concatenate([first, other], axis=1),
        jnp.concatenate([other, first], axis=1),
    )
    half_other = permute(half, swap)
    own = jnp.where(
        c == 0,
        jnp.concatenate([half, half_other], axis=1),
        jnp.concatenate([half_other, half], axis=1),
    )

    places = frames_in.reshape(NZ, NX, 8, D)
    places = lax.dynamic_slice(places, (0, 2 * c, 0, 2 * GROUP * y), (NZ, 2, 8, 2 * GROUP))
    low, high = places[..., :GROUP], places[..., GROUP:]
    low = jnp.where(c == 0, low, low[:, ::-1])
    high = jnp.where(c == 0, high[:, ::-1], high)
    packed = jnp.concatenate([low, high], axis=1).reshape(NZ * NX, 8, GROUP)
    spread = lax.all_to_all(packed, ("z", "x"), split_axis=0, concat_axis=0, tiled=True)
    spread = spread.reshape(1, TOKENS, GROUP)
    partner = permute(spread, lambda z, x, y, c: (z, 3 - x, y, c))
    both = jnp.where(
        group == 0,
        jnp.concatenate([spread, partner], axis=0),
        jnp.concatenate([partner, spread], axis=0),
    )
    pieces = [both] + [
        permute(both, lambda z, x, y, c, k=k: (z, x, y + k, c)) for k in (-1, 1, 2)
    ]

    mine, theirs = [], []
    block = own
    for t in range(1, 9):
        if t == 8:
            block = lax.dynamic_slice(block, (0, c * (ROWS // 2), 0), (3, ROWS // 2, GROUP))
        block = permute(block, ring)
        mine.append(block)
        theirs.append(permute(block, swap))

    place = jnp.stack([z, y, c]).astype(jnp.int32)
    output = project_and_attend(place, span_mask, own, mine, theirs, pieces)
    output = permute(output.reshape(FRAMES, 8, GROUP), home)
    output = lax.all_to_all(output, ("z", "x"), split_axis=0, concat_axis=0, tiled=True)
    return output.reshape(1, NZ * NX * 8, GROUP)


def solution(mesh):
    fine = Mesh(mesh.devices.reshape(NZ, NX, NY, NC), AXES)
    in_specs = (P(("z", "x"), None, None), P(("z", "x"), None, ("y", "c")), P())
    out_specs = P(("z", "x"), None, ("y", "c"))
    return jax.shard_map(
        per_device, mesh=fine, in_specs=in_specs, out_specs=out_specs, check_vma=False
    )
```

```python
import jax
import jax.numpy as jnp
from jax import lax
from jax.experimental import pallas as pl
from jax.experimental.pallas import tpu as pltpu
from jax.sharding import Mesh
from jax.sharding import PartitionSpec as P

D = 3072
HD = 128
FRAMES = 64
SPANS = 8
GROUP = 384
NZ, NX, NY, NC = 16, 4, 4, 2
AXES = ("z", "x", "y", "c")
SLICE = D // (NZ * NX)
TOKENS = FRAMES * 8


def permute(array, where_to):
    pairs = []
    for z in range(NZ):
        for x in range(NX):
            for y in range(NY):
                for c in range(NC):
                    a, b, d, e = where_to(z, x, y, c)
                    source = ((z * NX + x) * NY + y) * NC + c
                    pairs.append((source, (((a % NZ) * NX + b % NX) * NY + d % NY) * NC + e))
    return lax.ppermute(array, AXES, pairs)


def home(z, x, y, c):
    return (z, x, y, c) if c == x // 2 else (z, 3 - x, y, 1 - c)


def swap(z, x, y, c):
    return (z, x, y, 1 - c)


def pair(z, x, y, c):
    return (z, x ^ 1, y, c)


def ring(z, x, y, c):
    return (z + (1 if c == 0 else -1), x, y, c)


def one(t, near):
    return [(t, near, None)]


def two(t, near):
    return [(t, near, 0), (t, near, 1)]


def sent(near):
    return [
        one(0, near) + two(1, near) + two(2, near),
        two(3, near) + two(4, near),
        two(5, near) + two(6, near),
        two(7, near) + one(8, near),
    ]


def listing():
    s, r = sent(False), sent(True)
    own = [two(0, False)] + s + r
    swapped = [s[0] + r[0] + s[1], r[1] + s[2], r[2] + s[3], r[3]]
    return [(e, False) for e in own] + [(e, True) for e in swapped]


def attend_kernel(place, mask, *refs):
    blocks = listing()
    count = len(blocks)
    pieces = refs[count : count + 4]
    out = refs[count + 4]
    weights, tokens, qkv, bias, w_sems, x_sems = refs[count + 5 :]
    z, x, y, c = place[0], place[1], place[2], place[3]
    low = jnp.minimum(x, 3 - x)

    copies = []
    for i, (piece, shift) in enumerate(zip(pieces, (0, 1, 3, 2))):
        source = lax.rem(y + shift, NY)
        for half in range(2):
            at = pl.multiple_of((2 * source + half) * GROUP, GROUP)
            copies.append(
                pltpu.make_async_copy(piece.at[half], tokens.at[:, pl.ds(at, GROUP)], x_sems.at[2 * i + half])
            )
    done = set()
    for ref, (entries, swapped) in zip(refs[:count], blocks):
        owner = 1 - c if swapped else c
        sign = 1 - 2 * owner
        for k, (t, near, slot) in enumerate(entries):
            if t == 0 and not near and slot is None:
                continue
            key = (t, near, slot, swapped)
            assert key not in done
            done.add(key)
            from_z = lax.rem(z - sign * t + NZ, NZ)
            first = 1 - low if near else low
            high = owner if slot is None else slot
            from_x = first + high * (3 - 2 * first)
            row = pl.multiple_of((from_z * NX + from_x) * SLICE, SLICE)
            copies.append(
                pltpu.make_async_copy(ref.at[k], weights.at[:, pl.ds(row, SLICE)], w_sems.at[len(done) - 1])
            )
    assert len(done) == NZ * NX
    for copy in copies:
        copy.start()

    span_rows = TOKENS // SPANS
    column = lax.broadcasted_iota(jnp.int32, (1, TOKENS), 1)
    same = (
        lax.broadcasted_iota(jnp.int32, (span_rows, TOKENS), 0) & 7
    ) == (lax.broadcasted_iota(jnp.int32, (span_rows, TOKENS), 1) & 7)
    for i in range(SPANS):
        row = jnp.zeros((1, TOKENS), jnp.int32)
        for j in range(SPANS):
            row = jnp.where((column // span_rows) == j, mask[i, j], row)
        ok = same & (jnp.broadcast_to(row, (span_rows, TOKENS)) > 0)
        bias[pl.ds(i * span_rows, span_rows), :] = jnp.where(ok, 0.0, -1e30)

    for copy in copies:
        copy.wait()
    for j in range(3):
        for r in range(2):
            rows = pl.ds(r * (TOKENS // 2), TOKENS // 2)
            qkv[j, rows, :] = jnp.dot(
                tokens[rows, :], weights[j], preferred_element_type=jnp.float32
            ).astype(jnp.bfloat16)

    scale = 1.0 / jnp.sqrt(jnp.float32(HD))
    for h in range(GROUP // HD):
        lanes = pl.ds(h * HD, HD)
        for i in range(4):
            rows = pl.ds(i * 128, 128)
            width = (i + 1) * 128
            scores = lax.dot_general(
                qkv[0, rows, lanes],
                qkv[1, pl.ds(0, width), lanes],
                (((1,), (1,)), ((), ())),
                preferred_element_type=jnp.float32,
            )
            scores = scores * scale + bias[rows, pl.ds(0, width)]
            shares = jnp.exp(scores - jnp.max(scores, axis=-1, keepdims=True))
            total = jnp.sum(shares, axis=-1, keepdims=True)
            summed = jnp.dot(
                shares.astype(jnp.bfloat16),
                qkv[2, pl.ds(0, width), lanes],
                preferred_element_type=jnp.float32,
            )
            out[rows, lanes] = (summed / total).astype(jnp.bfloat16)


def project_and_attend(place, span_mask, blocks, pieces):
    arrays = [*blocks, *pieces]
    return pl.pallas_call(
        attend_kernel,
        out_shape=jax.ShapeDtypeStruct((TOKENS, GROUP), jnp.bfloat16),
        in_specs=[pl.BlockSpec(memory_space=pltpu.SMEM)] * 2
        + [pl.BlockSpec(memory_space=pl.ANY)] * len(arrays),
        out_specs=pl.BlockSpec(memory_space=pltpu.VMEM),
        scratch_shapes=[
            pltpu.VMEM((3, D, GROUP), jnp.bfloat16),
            pltpu.VMEM((TOKENS, D), jnp.bfloat16),
            pltpu.VMEM((3, TOKENS, GROUP), jnp.bfloat16),
            pltpu.VMEM((TOKENS, TOKENS), jnp.float32),
            pltpu.SemaphoreType.DMA((NZ * NX,)),
            pltpu.SemaphoreType.DMA((8,)),
        ],
        compiler_params=pltpu.CompilerParams(vmem_limit_bytes=20 * 1024 * 1024),
    )(place, span_mask, *arrays)


def join(*arrays):
    return jnp.concatenate(arrays, axis=0)


def per_device(frames_in, qkv_weight, span_mask):
    z, x, y, c = (lax.axis_index(name) for name in AXES)
    group = x // 2
    hold = lax.optimization_barrier

    places = frames_in.reshape(NZ, NX, 8, D)
    places = lax.dynamic_slice(places, (0, 2 * c, 0, 2 * GROUP * y), (NZ, 2, 8, 2 * GROUP))
    low, high = places[..., :GROUP], places[..., GROUP:]
    low = jnp.where(c == 0, low, low[:, ::-1])
    high = jnp.where(c == 0, high[:, ::-1], high)
    packed = jnp.concatenate([low, high], axis=1).reshape(NZ * NX, 8, GROUP)
    piece = jnp.transpose(qkv_weight, (1, 0, 2))[None]
    packed, piece = hold((packed, piece))
    spread = lax.all_to_all(packed, ("z", "x"), split_axis=0, concat_axis=0, tiled=True)

    first = permute(piece, home)
    first_other = permute(first, swap)
    own = jnp.where(c == 0, join(first, first_other), join(first_other, first))

    steps = [None]
    block = own
    batches, returned = [], []

    def step():
        nonlocal block
        if len(steps) == 8:
            block = lax.dynamic_slice(block, (c, 0, 0, 0), (1, 3, SLICE, GROUP))
        block = permute(block, ring)
        steps.append(block)

    def send(*parts):
        batch = join(*parts)
        batches.append(batch)
        returned.append(permute(batch, pair))

    step()
    step()
    block, spread = hold((block, spread))
    spread = spread.reshape(1, TOKENS, GROUP)
    partner = permute(spread, lambda z, x, y, c: (z, 3 - x, y, c))
    step()
    send(first, steps[1], steps[2])
    block, partner = hold((block, partner))
    both = jnp.where(group == 0, join(spread, partner), join(partner, spread))
    pieces = [both] + [
        permute(both, lambda z, x, y, c, k=k: (z, x, y + k, c)) for k in (-1, 1, 2)
    ]
    step()
    step()
    send(steps[3], steps[4])
    step()
    step()
    send(steps[5], steps[6])
    step()
    send(steps[7], steps[8])
    swapped = [
        join(batches[0], returned[0], batches[1]),
        join(returned[1], batches[2]),
        join(returned[2], batches[3]),
        returned[3],
    ]
    swapped = [permute(array, swap) for array in swapped]

    place = jnp.stack([z, x, y, c]).astype(jnp.int32)
    output = project_and_attend(place, span_mask, [own, *batches, *returned, *swapped], pieces)
    output = permute(output.reshape(FRAMES, 8, GROUP), home)
    output = lax.all_to_all(output, ("z", "x"), split_axis=0, concat_axis=0, tiled=True)
    return output.reshape(1, NZ * NX * 8, GROUP)


def solution(mesh):
    fine = Mesh(mesh.devices.reshape(NZ, NX, NY, NC), AXES)
    in_specs = (P(("z", "x"), None, None), P(("z", "x"), None, ("y", "c")), P())
    out_specs = P(("z", "x"), None, ("y", "c"))
    return jax.shard_map(
        per_device, mesh=fine, in_specs=in_specs, out_specs=out_specs, check_vma=False
    )
```

```python
import jax
import jax.numpy as jnp
from jax import lax
from jax.experimental import pallas as pl
from jax.experimental.pallas import tpu as pltpu
from jax.sharding import Mesh
from jax.sharding import PartitionSpec as P

D = 3072
HD = 128
FRAMES = 64
SPANS = 8
GROUP = 384
NZ, NX, NY, NC = 16, 4, 4, 2
AXES = ("z", "x", "y", "c")
SLICE = D // (NZ * NX)
TOKENS = FRAMES * 8


def permute(array, where_to):
    pairs = []
    for z in range(NZ):
        for x in range(NX):
            for y in range(NY):
                for c in range(NC):
                    a, b, d, e = where_to(z, x, y, c)
                    source = ((z * NX + x) * NY + y) * NC + c
                    pairs.append((source, (((a % NZ) * NX + b % NX) * NY + d % NY) * NC + e))
    return lax.ppermute(array, AXES, pairs)


def home(z, x, y, c):
    return (z, x, y, c) if c == x // 2 else (z, 3 - x, y, 1 - c)


def swap(z, x, y, c):
    return (z, x, y, 1 - c)


def pair(z, x, y, c):
    return (z, x ^ 1, y, c)


def along_z(k):
    return lambda z, x, y, c: (z + k, x, y, c)


FAR = (0, 4, -4, 8)
NEAR = (0, 1, -1, 2)


def attend_kernel(place, mask, *refs):
    count = 4 * len(NEAR)
    pieces = refs[count : count + 4]
    out = refs[count + 4]
    weights, tokens, qkv, bias, w_sems, x_sems = refs[count + 5 :]
    z, x, y, c = place[0], place[1], place[2], place[3]
    low = jnp.minimum(x, 3 - x)

    copies = []
    for i, (piece, shift) in enumerate(zip(pieces, (0, 1, 3, 2))):
        source = lax.rem(y + shift, NY)
        for half in range(2):
            at = pl.multiple_of((2 * source + half) * GROUP, GROUP)
            copies.append(
                pltpu.make_async_copy(piece.at[half], tokens.at[:, pl.ds(at, GROUP)], x_sems.at[2 * i + half])
            )
    for i, ref in enumerate(refs[:count]):
        shift = NEAR[i % 4]
        owner = 1 - c if i >= 8 else c
        first = 1 - low if i % 8 >= 4 else low
        from_x = first + owner * (3 - 2 * first)
        for k, far in enumerate(FAR):
            from_z = lax.rem(z - shift - far + 2 * NZ, NZ)
            row = pl.multiple_of((from_z * NX + from_x) * SLICE, SLICE)
            copies.append(
                pltpu.make_async_copy(ref.at[k], weights.at[:, pl.ds(row, SLICE)], w_sems.at[4 * i + k])
            )
    for copy in copies:
        copy.start()

    span_rows = TOKENS // SPANS
    column = lax.broadcasted_iota(jnp.int32, (1, TOKENS), 1)
    same = (
        lax.broadcasted_iota(jnp.int32, (span_rows, TOKENS), 0) & 7
    ) == (lax.broadcasted_iota(jnp.int32, (span_rows, TOKENS), 1) & 7)
    for i in range(SPANS):
        row = jnp.zeros((1, TOKENS), jnp.int32)
        for j in range(SPANS):
            row = jnp.where((column // span_rows) == j, mask[i, j], row)
        ok = same & (jnp.broadcast_to(row, (span_rows, TOKENS)) > 0)
        bias[pl.ds(i * span_rows, span_rows), :] = jnp.where(ok, 0.0, -1e30)

    for copy in copies:
        copy.wait()
    for j in range(3):
        for r in range(2):
            rows = pl.ds(r * (TOKENS // 2), TOKENS // 2)
            qkv[j, rows, :] = jnp.dot(
                tokens[rows, :], weights[j], preferred_element_type=jnp.float32
            ).astype(jnp.bfloat16)

    scale = 1.0 / jnp.sqrt(jnp.float32(HD))
    for h in range(GROUP // HD):
        lanes = pl.ds(h * HD, HD)
        for i in range(4):
            rows = pl.ds(i * 128, 128)
            width = (i + 1) * 128
            scores = lax.dot_general(
                qkv[0, rows, lanes],
                qkv[1, pl.ds(0, width), lanes],
                (((1,), (1,)), ((), ())),
                preferred_element_type=jnp.float32,
            )
            scores = scores * scale + bias[rows, pl.ds(0, width)]
            shares = jnp.exp(scores - jnp.max(scores, axis=-1, keepdims=True))
            total = jnp.sum(shares, axis=-1, keepdims=True)
            summed = jnp.dot(
                shares.astype(jnp.bfloat16),
                qkv[2, pl.ds(0, width), lanes],
                preferred_element_type=jnp.float32,
            )
            out[rows, lanes] = (summed / total).astype(jnp.bfloat16)


def project_and_attend(place, span_mask, blocks, pieces):
    arrays = [*blocks, *pieces]
    return pl.pallas_call(
        attend_kernel,
        out_shape=jax.ShapeDtypeStruct((TOKENS, GROUP), jnp.bfloat16),
        in_specs=[pl.BlockSpec(memory_space=pltpu.SMEM)] * 2
        + [pl.BlockSpec(memory_space=pl.ANY)] * len(arrays),
        out_specs=pl.BlockSpec(memory_space=pltpu.VMEM),
        scratch_shapes=[
            pltpu.VMEM((3, D, GROUP), jnp.bfloat16),
            pltpu.VMEM((TOKENS, D), jnp.bfloat16),
            pltpu.VMEM((3, TOKENS, GROUP), jnp.bfloat16),
            pltpu.VMEM((TOKENS, TOKENS), jnp.float32),
            pltpu.SemaphoreType.DMA((NZ * NX,)),
            pltpu.SemaphoreType.DMA((8,)),
        ],
        compiler_params=pltpu.CompilerParams(vmem_limit_bytes=20 * 1024 * 1024),
    )(place, span_mask, *arrays)


def join(*arrays):
    return jnp.concatenate(arrays, axis=0)


def per_device(frames_in, qkv_weight, span_mask):
    z, x, y, c = (lax.axis_index(name) for name in AXES)
    group = x // 2
    hold = lax.optimization_barrier

    places = frames_in.reshape(NZ, NX, 8, D)
    places = lax.dynamic_slice(places, (0, 2 * c, 0, 2 * GROUP * y), (NZ, 2, 8, 2 * GROUP))
    low, high = places[..., :GROUP], places[..., GROUP:]
    low = jnp.where(c == 0, low, low[:, ::-1])
    high = jnp.where(c == 0, high[:, ::-1], high)
    packed = jnp.concatenate([low, high], axis=1).reshape(NZ * NX, 8, GROUP)
    piece = jnp.transpose(qkv_weight, (1, 0, 2))[None]

    first = permute(piece, home)
    first, packed = hold((first, packed))
    far = join(first, *[permute(first, along_z(k)) for k in FAR[1:]])
    spread = lax.all_to_all(packed, ("z", "x"), split_axis=0, concat_axis=0, tiled=True)
    far_pair = permute(far, pair)
    near = [permute(far, along_z(k)) for k in NEAR[1:]]
    spread = spread.reshape(1, TOKENS, GROUP)
    partner = permute(spread, lambda z, x, y, c: (z, 3 - x, y, c))
    near[2], partner = hold((near[2], partner))
    both = jnp.where(group == 0, join(spread, partner), join(partner, spread))
    pieces = [both] + [
        permute(both, lambda z, x, y, c, k=k: (z, x, y + k, c)) for k in (-1, 1, 2)
    ]
    mine = [far, *near, far_pair] + [permute(block, pair) for block in near]
    mine[6], mine[7], *pieces[1:] = hold((mine[6], mine[7], *pieces[1:]))
    theirs = [permute(block, swap) for block in mine]

    place = jnp.stack([z, x, y, c]).astype(jnp.int32)
    output = project_and_attend(place, span_mask, [*mine, *theirs], pieces)
    output = permute(output.reshape(FRAMES, 8, GROUP), home)
    output = lax.all_to_all(output, ("z", "x"), split_axis=0, concat_axis=0, tiled=True)
    return output.reshape(1, NZ * NX * 8, GROUP)


def solution(mesh):
    fine = Mesh(mesh.devices.reshape(NZ, NX, NY, NC), AXES)
    in_specs = (P(("z", "x"), None, None), P(("z", "x"), None, ("y", "c")), P())
    out_specs = P(("z", "x"), None, ("y", "c"))
    return jax.shard_map(
        per_device, mesh=fine, in_specs=in_specs, out_specs=out_specs, check_vma=False
    )
```

```python
import jax
import jax.numpy as jnp
from jax import lax
from jax.experimental import pallas as pl
from jax.experimental.pallas import tpu as pltpu
from jax.sharding import Mesh
from jax.sharding import PartitionSpec as P

D = 3072
HD = 128
FRAMES = 64
SPANS = 8
GROUP = 384
NZ, NX, NY, NC = 16, 4, 4, 2
AXES = ("z", "x", "y", "c")
SLICE = D // (NZ * NX)
PART = 2 * SLICE
TOKENS = FRAMES * 8


def permute(array, where_to):
    pairs = []
    for z in range(NZ):
        for x in range(NX):
            for y in range(NY):
                for c in range(NC):
                    a, b, d, e = where_to(z, x, y, c)
                    source = ((z * NX + x) * NY + y) * NC + c
                    pairs.append((source, (((a % NZ) * NX + b % NX) * NY + d % NY) * NC + e))
    return lax.ppermute(array, AXES, pairs)


def home(z, x, y, c):
    return (z, x, y, c) if c == x // 2 else (z, 3 - x, y, 1 - c)


def second(z, x, y, c):
    near = x ^ 1
    return (z, near if x // 2 == c else 3 - near, y, x // 2)


def attend_kernel(place, mask, gathered, *refs):
    pieces, out = refs[:4], refs[4]
    weights, tokens, qkv, bias, w_sems, x_sems = refs[5:]
    y = place[0]

    copies = []
    for i, (piece, shift) in enumerate(zip(pieces, (0, 1, 3, 2))):
        source = lax.rem(y + shift, NY)
        for half in range(2):
            at = pl.multiple_of((2 * source + half) * GROUP, GROUP)
            copies.append(
                pltpu.make_async_copy(piece.at[half], tokens.at[:, pl.ds(at, GROUP)], x_sems.at[2 * i + half])
            )
    for i in range(D // PART):
        rows = pl.ds(i * PART, PART)
        copies.append(pltpu.make_async_copy(gathered.at[i], weights.at[:, rows], w_sems.at[i]))
    for copy in copies:
        copy.start()

    span_rows = TOKENS // SPANS
    column = lax.broadcasted_iota(jnp.int32, (1, TOKENS), 1)
    same = (
        lax.broadcasted_iota(jnp.int32, (span_rows, TOKENS), 0) & 7
    ) == (lax.broadcasted_iota(jnp.int32, (span_rows, TOKENS), 1) & 7)
    for i in range(SPANS):
        row = jnp.zeros((1, TOKENS), jnp.int32)
        for j in range(SPANS):
            row = jnp.where((column // span_rows) == j, mask[i, j], row)
        ok = same & (jnp.broadcast_to(row, (span_rows, TOKENS)) > 0)
        bias[pl.ds(i * span_rows, span_rows), :] = jnp.where(ok, 0.0, -1e30)

    for copy in copies:
        copy.wait()
    for j in range(3):
        for r in range(2):
            rows = pl.ds(r * (TOKENS // 2), TOKENS // 2)
            qkv[j, rows, :] = jnp.dot(
                tokens[rows, :], weights[j], preferred_element_type=jnp.float32
            ).astype(jnp.bfloat16)

    scale = 1.0 / jnp.sqrt(jnp.float32(HD))
    for h in range(GROUP // HD):
        lanes = pl.ds(h * HD, HD)
        for i in range(4):
            rows = pl.ds(i * 128, 128)
            width = (i + 1) * 128
            scores = lax.dot_general(
                qkv[0, rows, lanes],
                qkv[1, pl.ds(0, width), lanes],
                (((1,), (1,)), ((), ())),
                preferred_element_type=jnp.float32,
            )
            scores = scores * scale + bias[rows, pl.ds(0, width)]
            shares = jnp.exp(scores - jnp.max(scores, axis=-1, keepdims=True))
            total = jnp.sum(shares, axis=-1, keepdims=True)
            summed = jnp.dot(
                shares.astype(jnp.bfloat16),
                qkv[2, pl.ds(0, width), lanes],
                preferred_element_type=jnp.float32,
            )
            out[rows, lanes] = (summed / total).astype(jnp.bfloat16)


def project_and_attend(place, span_mask, gathered, pieces):
    arrays = [gathered, *pieces]
    return pl.pallas_call(
        attend_kernel,
        out_shape=jax.ShapeDtypeStruct((TOKENS, GROUP), jnp.bfloat16),
        in_specs=[pl.BlockSpec(memory_space=pltpu.SMEM)] * 2
        + [pl.BlockSpec(memory_space=pl.ANY)] * len(arrays),
        out_specs=pl.BlockSpec(memory_space=pltpu.VMEM),
        scratch_shapes=[
            pltpu.VMEM((3, D, GROUP), jnp.bfloat16),
            pltpu.VMEM((TOKENS, D), jnp.bfloat16),
            pltpu.VMEM((3, TOKENS, GROUP), jnp.bfloat16),
            pltpu.VMEM((TOKENS, TOKENS), jnp.float32),
            pltpu.SemaphoreType.DMA((D // PART,)),
            pltpu.SemaphoreType.DMA((8,)),
        ],
        compiler_params=pltpu.CompilerParams(vmem_limit_bytes=20 * 1024 * 1024),
    )(place, span_mask, *arrays)


def join(*arrays):
    return jnp.concatenate(arrays, axis=0)


def per_device(frames_in, qkv_weight, span_mask):
    z, x, y, c = (lax.axis_index(name) for name in AXES)
    group = x // 2
    hold = lax.optimization_barrier

    places = frames_in.reshape(NZ, NX, 8, D)
    places = lax.dynamic_slice(places, (0, 2 * c, 0, 2 * GROUP * y), (NZ, 2, 8, 2 * GROUP))
    low, high = places[..., :GROUP], places[..., GROUP:]
    low = jnp.where(c == 0, low, low[:, ::-1])
    high = jnp.where(c == 0, high[:, ::-1], high)
    packed = jnp.concatenate([low, high], axis=1).reshape(NZ * NX, 8, GROUP)

    piece = jnp.transpose(qkv_weight, (1, 0, 2))
    first = permute(piece, home)
    other = permute(piece, second)
    slot = jnp.where(c == group, x, 3 - x)
    half = jnp.where(
        slot % 2 == 0,
        jnp.concatenate([first, other], axis=1),
        jnp.concatenate([other, first], axis=1),
    )
    half, packed = hold((half, packed))
    gathered = lax.all_gather(half[None], ("z", "c"), axis=0, tiled=True)
    spread = lax.all_to_all(packed, ("z", "x"), split_axis=0, concat_axis=0, tiled=True)
    spread = spread.reshape(1, TOKENS, GROUP)
    partner = permute(spread, lambda z, x, y, c: (z, 3 - x, y, c))
    both = jnp.where(group == 0, join(spread, partner), join(partner, spread))
    pieces = [both] + [
        permute(both, lambda z, x, y, c, k=k: (z, x, y + k, c)) for k in (-1, 1, 2)
    ]
    place = jnp.stack([y]).astype(jnp.int32)
    output = project_and_attend(place, span_mask, gathered, pieces)
    output = permute(output.reshape(FRAMES, 8, GROUP), home)
    output = lax.all_to_all(output, ("z", "x"), split_axis=0, concat_axis=0, tiled=True)
    return output.reshape(1, NZ * NX * 8, GROUP)


def solution(mesh):
    fine = Mesh(mesh.devices.reshape(NZ, NX, NY, NC), AXES)
    in_specs = (P(("z", "x"), None, None), P(("z", "x"), None, ("y", "c")), P())
    out_specs = P(("z", "x"), None, ("y", "c"))
    return jax.shard_map(
        per_device, mesh=fine, in_specs=in_specs, out_specs=out_specs, check_vma=False
    )
```

```python
import jax
import jax.numpy as jnp
from jax import lax
from jax.experimental import pallas as pl
from jax.experimental.pallas import tpu as pltpu
from jax.sharding import Mesh
from jax.sharding import PartitionSpec as P

D = 3072
HD = 128
FRAMES = 64
SPANS = 8
GROUP = 384
NZ, NX, NY, NC = 16, 4, 4, 2
AXES = ("z", "x", "y", "c")
SLICE = D // (NZ * NX)
PART = 2 * SLICE
CHUNK = D // 4
SHIFTS = (0, 1, 3, 2)
TOKENS = FRAMES * 8


def permute(array, where_to):
    pairs = []
    for z in range(NZ):
        for x in range(NX):
            for y in range(NY):
                for c in range(NC):
                    a, b, d, e = where_to(z, x, y, c)
                    source = ((z * NX + x) * NY + y) * NC + c
                    pairs.append((source, (((a % NZ) * NX + b % NX) * NY + d % NY) * NC + e))
    return lax.ppermute(array, AXES, pairs)


def home(z, x, y, c):
    return (z, x, y, c) if c == x // 2 else (z, 3 - x, y, 1 - c)


def second(z, x, y, c):
    near = x ^ 1
    return (z, near if x // 2 == c else 3 - near, y, x // 2)


def attend_kernel(place, mask, gathered, *refs):
    pieces, out = refs[:8], refs[8]
    weights, tokens, sums, qkv, bias, w_sems, x_sems = refs[9:]
    y, group = place[0], place[1]

    token_copies = []
    for i, piece in enumerate(pieces):
        source = lax.rem(y + SHIFTS[i // 2], NY)
        half = group if i % 2 == 0 else 1 - group
        at = pl.multiple_of((2 * source + half) * GROUP, GROUP)
        token_copies.append(pltpu.make_async_copy(piece, tokens.at[:, pl.ds(at, GROUP)], x_sems.at[i]))
    weight_copies = []
    for i in range(D // PART):
        rows = pl.ds(i * PART, PART)
        weight_copies.append(pltpu.make_async_copy(gathered.at[i], weights.at[:, rows], w_sems.at[i]))
    for copy in token_copies + weight_copies:
        copy.start()

    span_rows = TOKENS // SPANS
    column = lax.broadcasted_iota(jnp.int32, (1, TOKENS), 1)
    same = (
        lax.broadcasted_iota(jnp.int32, (span_rows, TOKENS), 0) & 7
    ) == (lax.broadcasted_iota(jnp.int32, (span_rows, TOKENS), 1) & 7)
    for i in range(SPANS):
        row = jnp.zeros((1, TOKENS), jnp.int32)
        for j in range(SPANS):
            row = jnp.where((column // span_rows) == j, mask[i, j], row)
        ok = same & (jnp.broadcast_to(row, (span_rows, TOKENS)) > 0)
        bias[pl.ds(i * span_rows, span_rows), :] = jnp.where(ok, 0.0, -1e30)

    for copy in token_copies:
        copy.wait()
    per_chunk = CHUNK // PART
    for chunk in range(D // CHUNK):
        for copy in weight_copies[chunk * per_chunk : (chunk + 1) * per_chunk]:
            copy.wait()
        features = pl.ds(chunk * CHUNK, CHUNK)
        for j in range(3):
            product = jnp.dot(
                tokens[:, features], weights[j, features, :], preferred_element_type=jnp.float32
            )
            if chunk:
                product = sums[j] + product
            if chunk < D // CHUNK - 1:
                sums[j] = product
            else:
                qkv[j] = product.astype(jnp.bfloat16)

    scale = 1.0 / jnp.sqrt(jnp.float32(HD))
    for h in range(GROUP // HD):
        lanes = pl.ds(h * HD, HD)
        for i in range(4):
            rows = pl.ds(i * 128, 128)
            width = (i + 1) * 128
            scores = lax.dot_general(
                qkv[0, rows, lanes],
                qkv[1, pl.ds(0, width), lanes],
                (((1,), (1,)), ((), ())),
                preferred_element_type=jnp.float32,
            )
            scores = scores * scale + bias[rows, pl.ds(0, width)]
            shares = jnp.exp(scores - jnp.max(scores, axis=-1, keepdims=True))
            total = jnp.sum(shares, axis=-1, keepdims=True)
            summed = jnp.dot(
                shares.astype(jnp.bfloat16),
                qkv[2, pl.ds(0, width), lanes],
                preferred_element_type=jnp.float32,
            )
            out[rows, lanes] = (summed / total).astype(jnp.bfloat16)


def project_and_attend(place, span_mask, gathered, pieces):
    arrays = [gathered, *pieces]
    return pl.pallas_call(
        attend_kernel,
        out_shape=jax.ShapeDtypeStruct((TOKENS, GROUP), jnp.bfloat16),
        in_specs=[pl.BlockSpec(memory_space=pltpu.SMEM)] * 2
        + [pl.BlockSpec(memory_space=pl.ANY)] * len(arrays),
        out_specs=pl.BlockSpec(memory_space=pltpu.VMEM),
        scratch_shapes=[
            pltpu.VMEM((3, D, GROUP), jnp.bfloat16),
            pltpu.VMEM((TOKENS, D), jnp.bfloat16),
            pltpu.VMEM((3, TOKENS, GROUP), jnp.float32),
            pltpu.VMEM((3, TOKENS, GROUP), jnp.bfloat16),
            pltpu.VMEM((TOKENS, TOKENS), jnp.float32),
            pltpu.SemaphoreType.DMA((D // PART,)),
            pltpu.SemaphoreType.DMA((8,)),
        ],
        compiler_params=pltpu.CompilerParams(vmem_limit_bytes=44 * 1024 * 1024),
    )(place, span_mask, *arrays)


def per_device(frames_in, qkv_weight, span_mask):
    z, x, y, c = (lax.axis_index(name) for name in AXES)
    group = x // 2
    hold = lax.optimization_barrier

    places = frames_in.reshape(NZ, NX, 8, D)
    places = lax.dynamic_slice(places, (0, 2 * c, 0, 2 * GROUP * y), (NZ, 2, 8, 2 * GROUP))
    low, high = places[..., :GROUP], places[..., GROUP:]
    low = jnp.where(c == 0, low, low[:, ::-1])
    high = jnp.where(c == 0, high[:, ::-1], high)
    packed = jnp.concatenate([low, high], axis=1).reshape(NZ * NX, 8, GROUP)

    piece = jnp.transpose(qkv_weight, (1, 0, 2))
    first = permute(piece, home)
    other = permute(piece, second)
    slot = jnp.where(c == group, x, 3 - x)
    half = jnp.where(
        slot % 2 == 0,
        jnp.concatenate([first, other], axis=1),
        jnp.concatenate([other, first], axis=1),
    )
    half, packed = hold((half, packed))
    gathered = lax.all_gather(half[None], ("z", "c"), axis=0, tiled=True)
    spread = lax.all_to_all(packed, ("z", "x"), split_axis=0, concat_axis=0, tiled=True)
    spread = spread.reshape(TOKENS, GROUP)
    partner = permute(spread, lambda z, x, y, c: (z, 3 - x, y, c))
    pieces = [spread, partner]
    for shift in SHIFTS[1:]:
        for block in (spread, partner):
            pieces.append(permute(block, lambda z, x, y, c, k=shift: (z, x, y - k, c)))

    place = jnp.stack([y, group]).astype(jnp.int32)
    output = project_and_attend(place, span_mask, gathered, pieces)
    output = permute(output.reshape(FRAMES, 8, GROUP), home)
    output = lax.all_to_all(output, ("z", "x"), split_axis=0, concat_axis=0, tiled=True)
    return output.reshape(1, NZ * NX * 8, GROUP)


def solution(mesh):
    fine = Mesh(mesh.devices.reshape(NZ, NX, NY, NC), AXES)
    in_specs = (P(("z", "x"), None, None), P(("z", "x"), None, ("y", "c")), P())
    out_specs = P(("z", "x"), None, ("y", "c"))
    return jax.shard_map(
        per_device, mesh=fine, in_specs=in_specs, out_specs=out_specs, check_vma=False
    )
```

```python
import functools

import jax
import jax.numpy as jnp
from jax import lax
from jax.experimental import pallas as pl
from jax.experimental.pallas import tpu as pltpu
from jax.sharding import Mesh
from jax.sharding import PartitionSpec as P

D = 3072
HD = 128
FRAMES = 64
SPANS = 8
GROUP = 384
NZ, NX, NY, NC = 16, 4, 4, 2
AXES = ("z", "x", "y", "c")
SLICE = D // (NZ * NX)
PART = 2 * SLICE
CHUNK = D // 4
SHIFTS = (0, 1, 3, 2)
TOKENS = FRAMES * 8


def permute(array, where_to):
    pairs = []
    for z in range(NZ):
        for x in range(NX):
            for y in range(NY):
                for c in range(NC):
                    a, b, d, e = where_to(z, x, y, c)
                    source = ((z * NX + x) * NY + y) * NC + c
                    pairs.append((source, (((a % NZ) * NX + b % NX) * NY + d % NY) * NC + e))
    return lax.ppermute(array, AXES, pairs)


def home(z, x, y, c, k=0):
    return (z, (x if c == x // 2 else 3 - x) ^ k, y, x // 2)


def second(z, x, y, c):
    near = x ^ 1
    return (z, near if x // 2 == c else 3 - near, y, x // 2)


def attend_kernel(place, mask, gathered, *refs):
    pieces, outs = refs[:8], refs[8:12]
    weights, tokens, sums, qkv, bias, result, w_sems, x_sems = refs[12:]
    y, group, place_x = place[0], place[1], place[2]

    token_copies = []
    for i, piece in enumerate(pieces):
        source = lax.rem(y + SHIFTS[i // 2], NY)
        half = group if i % 2 == 0 else 1 - group
        at = pl.multiple_of((2 * source + half) * GROUP, GROUP)
        token_copies.append(pltpu.make_async_copy(piece, tokens.at[:, pl.ds(at, GROUP)], x_sems.at[i]))
    weight_copies = []
    for i in range(D // PART):
        rows = pl.ds(i * PART, PART)
        weight_copies.append(pltpu.make_async_copy(gathered.at[i], weights.at[:, rows], w_sems.at[i]))
    for copy in token_copies + weight_copies:
        copy.start()

    span_rows = TOKENS // SPANS
    column = lax.broadcasted_iota(jnp.int32, (1, TOKENS), 1)
    same = (
        lax.broadcasted_iota(jnp.int32, (span_rows, TOKENS), 0) & 7
    ) == (lax.broadcasted_iota(jnp.int32, (span_rows, TOKENS), 1) & 7)
    for i in range(SPANS):
        row = jnp.zeros((1, TOKENS), jnp.int32)
        for j in range(SPANS):
            row = jnp.where((column // span_rows) == j, mask[i, j], row)
        ok = same & (jnp.broadcast_to(row, (span_rows, TOKENS)) > 0)
        bias[pl.ds(i * span_rows, span_rows), :] = jnp.where(ok, 0.0, -1e30)

    for copy in token_copies:
        copy.wait()
    per_chunk = CHUNK // PART
    for chunk in range(D // CHUNK):
        for copy in weight_copies[chunk * per_chunk : (chunk + 1) * per_chunk]:
            copy.wait()
        features = pl.ds(chunk * CHUNK, CHUNK)
        for j in range(3):
            product = jnp.dot(
                tokens[:, features], weights[j, features, :], preferred_element_type=jnp.float32
            )
            if chunk:
                product = sums[j] + product
            if chunk < D // CHUNK - 1:
                sums[j] = product
            else:
                qkv[j] = product.astype(jnp.bfloat16)

    scale = 1.0 / jnp.sqrt(jnp.float32(HD))
    for h in range(GROUP // HD):
        lanes = pl.ds(h * HD, HD)
        for i in range(4):
            rows = pl.ds(i * 128, 128)
            width = (i + 1) * 128
            scores = lax.dot_general(
                qkv[0, rows, lanes],
                qkv[1, pl.ds(0, width), lanes],
                (((1,), (1,)), ((), ())),
                preferred_element_type=jnp.float32,
            )
            scores = scores * scale + bias[rows, pl.ds(0, width)]
            shares = jnp.exp(scores - jnp.max(scores, axis=-1, keepdims=True))
            total = jnp.sum(shares, axis=-1, keepdims=True)
            summed = jnp.dot(
                shares.astype(jnp.bfloat16),
                qkv[2, pl.ds(0, width), lanes],
                preferred_element_type=jnp.float32,
            )
            attended = (summed / total).reshape(4, NX, 8, HD)
            for to_x in range(NX):
                part = attended[:, to_x].reshape(32, HD)
                result[to_x, pl.ds(i * 32, 32), lanes] = part.astype(jnp.bfloat16)
    for k, out in enumerate(outs):
        out[...] = result[place_x ^ k]


def project_and_attend(place, span_mask, gathered, pieces):
    arrays = [gathered, *pieces]
    return pl.pallas_call(
        attend_kernel,
        out_shape=[jax.ShapeDtypeStruct((TOKENS // NX, GROUP), jnp.bfloat16)] * NX,
        in_specs=[pl.BlockSpec(memory_space=pltpu.SMEM)] * 2
        + [pl.BlockSpec(memory_space=pl.ANY)] * len(arrays),
        out_specs=[pl.BlockSpec(memory_space=pltpu.VMEM)] * NX,
        scratch_shapes=[
            pltpu.VMEM((3, D, GROUP), jnp.bfloat16),
            pltpu.VMEM((TOKENS, D), jnp.bfloat16),
            pltpu.VMEM((3, TOKENS, GROUP), jnp.float32),
            pltpu.VMEM((3, TOKENS, GROUP), jnp.bfloat16),
            pltpu.VMEM((TOKENS, TOKENS), jnp.float32),
            pltpu.VMEM((NX, TOKENS // NX, GROUP), jnp.bfloat16),
            pltpu.SemaphoreType.DMA((D // PART,)),
            pltpu.SemaphoreType.DMA((8,)),
        ],
        compiler_params=pltpu.CompilerParams(vmem_limit_bytes=44 * 1024 * 1024),
    )(place, span_mask, *arrays)


def per_device(frames_in, qkv_weight, span_mask):
    z, x, y, c = (lax.axis_index(name) for name in AXES)
    group = x // 2
    hold = lax.optimization_barrier

    places = frames_in.reshape(NZ, NX, 8, D)
    places = lax.dynamic_slice(places, (0, 2 * c, 0, 2 * GROUP * y), (NZ, 2, 8, 2 * GROUP))
    low, high = places[..., :GROUP], places[..., GROUP:]
    low = jnp.where(c == 0, low, low[:, ::-1])
    high = jnp.where(c == 0, high[:, ::-1], high)
    packed = jnp.concatenate([low, high], axis=1).reshape(NZ * NX, 8, GROUP)

    piece = jnp.transpose(qkv_weight, (1, 0, 2))
    first = permute(piece, home)
    other = permute(piece, second)
    slot = jnp.where(c == group, x, 3 - x)
    half = jnp.where(
        slot % 2 == 0,
        jnp.concatenate([first, other], axis=1),
        jnp.concatenate([other, first], axis=1),
    )
    half, packed = hold((half, packed))
    gathered = lax.all_gather(half[None], ("z", "c"), axis=0, tiled=True)
    spread = lax.all_to_all(packed, ("z", "x"), split_axis=0, concat_axis=0, tiled=True)
    spread = spread.reshape(TOKENS, GROUP)
    partner = permute(spread, lambda z, x, y, c: (z, 3 - x, y, c))
    pieces = [spread, partner]
    for shift in SHIFTS[1:]:
        for block in (spread, partner):
            pieces.append(permute(block, lambda z, x, y, c, k=shift: (z, x, y - k, c)))

    place = jnp.stack([y, group, slot]).astype(jnp.int32)
    parts = project_and_attend(place, span_mask, gathered, pieces)
    parts = [permute(part, functools.partial(home, k=k)) for k, part in enumerate(parts)]
    parts = [lax.select_n(x, *[parts[k ^ at] for k in range(NX)]) for at in range(NX)]
    output = jnp.stack([part.reshape(NZ, 8, GROUP) for part in parts], axis=1)
    output = lax.all_to_all(output, "z", split_axis=0, concat_axis=0, tiled=True)
    return output.reshape(1, NZ * NX * 8, GROUP)


def solution(mesh):
    fine = Mesh(mesh.devices.reshape(NZ, NX, NY, NC), AXES)
    in_specs = (P(("z", "x"), None, None), P(("z", "x"), None, ("y", "c")), P())
    out_specs = P(("z", "x"), None, ("y", "c"))
    return jax.shard_map(
        per_device, mesh=fine, in_specs=in_specs, out_specs=out_specs, check_vma=False
    )
```

```python
import functools

import jax
import jax.numpy as jnp
from jax import lax
from jax.experimental import pallas as pl
from jax.experimental.pallas import tpu as pltpu
from jax.sharding import Mesh
from jax.sharding import PartitionSpec as P

D = 3072
HD = 128
FRAMES = 64
SPANS = 8
GROUP = 384
NZ, NX, NY, NC = 16, 4, 4, 2
AXES = ("z", "x", "y", "c")
SLICE = D // (NZ * NX)
PART = 2 * SLICE
CHUNK = D // 2
SHIFTS = (0, 1, 3, 2)
TOKENS = FRAMES * 8


def permute(array, where_to):
    pairs = []
    for z in range(NZ):
        for x in range(NX):
            for y in range(NY):
                for c in range(NC):
                    a, b, d, e = where_to(z, x, y, c)
                    source = ((z * NX + x) * NY + y) * NC + c
                    pairs.append((source, (((a % NZ) * NX + b % NX) * NY + d % NY) * NC + e))
    return lax.ppermute(array, AXES, pairs)


def home(z, x, y, c, k=0):
    return (z, (x if c == x // 2 else 3 - x) ^ k, y, x // 2)


def second(z, x, y, c):
    near = x ^ 1
    return (z, near if x // 2 == c else 3 - near, y, x // 2)


def attend_kernel(place, mask, gathered, *refs):
    pieces, outs = refs[:8], refs[8:12]
    weights, tokens, sums, qkv, bias, result, w_sems, x_sems = refs[12:]
    y, group, place_x = place[0], place[1], place[2]

    token_copies = []
    for i, piece in enumerate(pieces):
        source = lax.rem(y + SHIFTS[i // 2], NY)
        half = group if i % 2 == 0 else 1 - group
        at = pl.multiple_of((2 * source + half) * GROUP, GROUP)
        token_copies.append(pltpu.make_async_copy(piece, tokens.at[:, pl.ds(at, GROUP)], x_sems.at[i]))
    weight_copies = []
    for i in range(D // PART):
        rows = pl.ds(i * PART, PART)
        for j in range(3):
            lanes = pl.ds(j * GROUP, GROUP)
            weight_copies.append(
                pltpu.make_async_copy(gathered.at[i, j], weights.at[rows, lanes], w_sems.at[i, j])
            )
    for copy in token_copies + weight_copies:
        copy.start()

    span_rows = TOKENS // SPANS
    column = lax.broadcasted_iota(jnp.int32, (1, TOKENS), 1)
    same = (
        lax.broadcasted_iota(jnp.int32, (span_rows, TOKENS), 0) & 7
    ) == (lax.broadcasted_iota(jnp.int32, (span_rows, TOKENS), 1) & 7)
    for i in range(SPANS):
        row = jnp.zeros((1, TOKENS), jnp.int32)
        for j in range(SPANS):
            row = jnp.where((column // span_rows) == j, mask[i, j], row)
        ok = same & (jnp.broadcast_to(row, (span_rows, TOKENS)) > 0)
        bias[pl.ds(i * span_rows, span_rows), :] = jnp.where(ok, 0.0, -1e30)

    for copy in token_copies:
        copy.wait()
    per_chunk = 3 * CHUNK // PART
    for chunk in range(D // CHUNK):
        for copy in weight_copies[chunk * per_chunk : (chunk + 1) * per_chunk]:
            copy.wait()
        features = pl.ds(chunk * CHUNK, CHUNK)
        product = jnp.dot(
            tokens[:, features], weights[features, :], preferred_element_type=jnp.float32
        )
        if chunk:
            product = sums[...] + product
        if chunk < D // CHUNK - 1:
            sums[...] = product
        else:
            qkv[...] = product.astype(jnp.bfloat16)

    scale = 1.0 / jnp.sqrt(jnp.float32(HD))
    heads = range(GROUP // HD)
    for i in range(4):
        rows = pl.ds(i * 128, 128)
        keys = pl.ds(0, (i + 1) * 128)
        scores = [
            lax.dot_general(
                qkv[rows, pl.ds(h * HD, HD)],
                qkv[keys, pl.ds(GROUP + h * HD, HD)],
                (((1,), (1,)), ((), ())),
                preferred_element_type=jnp.float32,
            )
            for h in heads
        ]
        scores = [s * scale + bias[rows, keys] for s in scores]
        shares = [jnp.exp(s - jnp.max(s, axis=-1, keepdims=True)) for s in scores]
        totals = [jnp.sum(s, axis=-1, keepdims=True) for s in shares]
        summed = [
            jnp.dot(
                s.astype(jnp.bfloat16),
                qkv[keys, pl.ds(2 * GROUP + h * HD, HD)],
                preferred_element_type=jnp.float32,
            )
            for h, s in zip(heads, shares)
        ]
        for h in heads:
            attended = (summed[h] / totals[h]).reshape(4, NX, 8, HD)
            for to_x in range(NX):
                part = attended[:, to_x].reshape(32, HD)
                result[to_x, pl.ds(i * 32, 32), pl.ds(h * HD, HD)] = part.astype(jnp.bfloat16)
    for k, out in enumerate(outs):
        out[...] = result[place_x ^ k]


def project_and_attend(place, span_mask, gathered, pieces):
    arrays = [gathered, *pieces]
    return pl.pallas_call(
        attend_kernel,
        out_shape=[jax.ShapeDtypeStruct((TOKENS // NX, GROUP), jnp.bfloat16)] * NX,
        in_specs=[pl.BlockSpec(memory_space=pltpu.SMEM)] * 2
        + [pl.BlockSpec(memory_space=pl.ANY)] * len(arrays),
        out_specs=[pl.BlockSpec(memory_space=pltpu.VMEM)] * NX,
        scratch_shapes=[
            pltpu.VMEM((D, 3 * GROUP), jnp.bfloat16),
            pltpu.VMEM((TOKENS, D), jnp.bfloat16),
            pltpu.VMEM((TOKENS, 3 * GROUP), jnp.float32),
            pltpu.VMEM((TOKENS, 3 * GROUP), jnp.bfloat16),
            pltpu.VMEM((TOKENS, TOKENS), jnp.float32),
            pltpu.VMEM((NX, TOKENS // NX, GROUP), jnp.bfloat16),
            pltpu.SemaphoreType.DMA((D // PART, 3)),
            pltpu.SemaphoreType.DMA((8,)),
        ],
        compiler_params=pltpu.CompilerParams(vmem_limit_bytes=44 * 1024 * 1024),
    )(place, span_mask, *arrays)


def per_device(frames_in, qkv_weight, span_mask):
    z, x, y, c = (lax.axis_index(name) for name in AXES)
    group = x // 2
    hold = lax.optimization_barrier

    places = frames_in.reshape(NZ, NX, 8, D)
    places = lax.dynamic_slice(places, (0, 2 * c, 0, 2 * GROUP * y), (NZ, 2, 8, 2 * GROUP))
    low, high = places[..., :GROUP], places[..., GROUP:]
    low = jnp.where(c == 0, low, low[:, ::-1])
    high = jnp.where(c == 0, high[:, ::-1], high)
    packed = jnp.concatenate([low, high], axis=1).reshape(NZ * NX, 8, GROUP)

    piece = jnp.transpose(qkv_weight, (1, 0, 2))
    first = permute(piece, home)
    other = permute(piece, second)
    slot = jnp.where(c == group, x, 3 - x)
    half = jnp.where(
        slot % 2 == 0,
        jnp.concatenate([first, other], axis=1),
        jnp.concatenate([other, first], axis=1),
    )
    half, packed = hold((half, packed))
    gathered = lax.all_gather(half[None], ("z", "c"), axis=0, tiled=True)
    spread = lax.all_to_all(packed, ("z", "x"), split_axis=0, concat_axis=0, tiled=True)
    spread = spread.reshape(TOKENS, GROUP)
    partner = permute(spread, lambda z, x, y, c: (z, 3 - x, y, c))
    pieces = [spread, partner]
    for shift in SHIFTS[1:]:
        for block in (spread, partner):
            pieces.append(permute(block, lambda z, x, y, c, k=shift: (z, x, y - k, c)))

    place = jnp.stack([y, group, slot]).astype(jnp.int32)
    parts = project_and_attend(place, span_mask, gathered, pieces)
    parts = [permute(part, functools.partial(home, k=k)) for k, part in enumerate(parts)]
    parts = [lax.select_n(x, *[parts[k ^ at] for k in range(NX)]) for at in range(NX)]
    output = jnp.stack([part.reshape(NZ, 8, GROUP) for part in parts], axis=1)
    output = lax.all_to_all(output, "z", split_axis=0, concat_axis=0, tiled=True)
    return output.reshape(1, NZ * NX * 8, GROUP)


def solution(mesh):
    fine = Mesh(mesh.devices.reshape(NZ, NX, NY, NC), AXES)
    in_specs = (P(("z", "x"), None, None), P(("z", "x"), None, ("y", "c")), P())
    out_specs = P(("z", "x"), None, ("y", "c"))
    return jax.shard_map(
        per_device, mesh=fine, in_specs=in_specs, out_specs=out_specs, check_vma=False
    )
```

```python
import functools

import jax
import jax.numpy as jnp
from jax import lax
from jax.experimental import pallas as pl
from jax.experimental.pallas import tpu as pltpu
from jax.sharding import Mesh
from jax.sharding import PartitionSpec as P

D = 3072
HD = 128
FRAMES = 64
SPANS = 8
GROUP = 384
NZ, NX, NY, NC = 16, 4, 4, 2
AXES = ("z", "x", "y", "c")
SLICE = D // (NZ * NX)
PART = 2 * SLICE
CHUNK = D // 4
SHIFTS = (0, 1, 3, 2)
TOKENS = FRAMES * 8


def permute(array, where_to):
    pairs = []
    for z in range(NZ):
        for x in range(NX):
            for y in range(NY):
                for c in range(NC):
                    a, b, d, e = where_to(z, x, y, c)
                    source = ((z * NX + x) * NY + y) * NC + c
                    pairs.append((source, (((a % NZ) * NX + b % NX) * NY + d % NY) * NC + e))
    return lax.ppermute(array, AXES, pairs)


def home(z, x, y, c, k=0):
    return (z, (x if c == x // 2 else 3 - x) ^ k, y, x // 2)


def second(z, x, y, c):
    near = x ^ 1
    return (z, near if x // 2 == c else 3 - near, y, x // 2)


def attend_kernel(place, mask, gathered, *refs):
    pieces, outs = refs[:8], refs[8:12]
    weights, tokens, sums, qkv, bias, result, w_sems, x_sems = refs[12:]
    y, group, place_x = place[0], place[1], place[2]

    token_copies = []
    for i, piece in enumerate(pieces):
        source = lax.rem(y + SHIFTS[i // 2], NY)
        half = group if i % 2 == 0 else 1 - group
        at = pl.multiple_of((2 * source + half) * GROUP, GROUP)
        token_copies.append(pltpu.make_async_copy(piece, tokens.at[:, pl.ds(at, GROUP)], x_sems.at[i]))
    weight_copies = []
    for chunk in range(D // CHUNK):
        parts = pl.ds(chunk * (CHUNK // PART), CHUNK // PART)
        for j in range(3):
            lanes = pl.ds(j * GROUP, GROUP)
            weight_copies.append(
                pltpu.make_async_copy(
                    gathered.at[parts, j], weights.at[parts, :, lanes], w_sems.at[chunk, j]
                )
            )
    for copy in token_copies + weight_copies:
        copy.start()

    span_rows = TOKENS // SPANS
    column = lax.broadcasted_iota(jnp.int32, (1, TOKENS), 1)
    same = (
        lax.broadcasted_iota(jnp.int32, (span_rows, TOKENS), 0) & 7
    ) == (lax.broadcasted_iota(jnp.int32, (span_rows, TOKENS), 1) & 7)
    for i in range(SPANS):
        row = jnp.zeros((1, TOKENS), jnp.int32)
        for j in range(SPANS):
            row = jnp.where((column // span_rows) == j, mask[i, j], row)
        ok = same & (jnp.broadcast_to(row, (span_rows, TOKENS)) > 0)
        bias[pl.ds(i * span_rows, span_rows), :] = jnp.where(ok, 0.0, -1e30)

    for copy in token_copies:
        copy.wait()
    for chunk in range(D // CHUNK):
        for copy in weight_copies[3 * chunk : 3 * chunk + 3]:
            copy.wait()
        features = pl.ds(chunk * CHUNK, CHUNK)
        parts = pl.ds(chunk * (CHUNK // PART), CHUNK // PART)
        product = jnp.dot(
            tokens[:, features],
            weights[parts].reshape(CHUNK, 3 * GROUP),
            preferred_element_type=jnp.float32,
        )
        if chunk:
            product = sums[...] + product
        if chunk < D // CHUNK - 1:
            sums[...] = product
        else:
            qkv[...] = product.astype(jnp.bfloat16)

    scale = 1.0 / jnp.sqrt(jnp.float32(HD))
    heads = range(GROUP // HD)
    for i in range(4):
        rows = pl.ds(i * 128, 128)
        keys = pl.ds(0, (i + 1) * 128)
        scores = [
            lax.dot_general(
                qkv[rows, pl.ds(h * HD, HD)],
                qkv[keys, pl.ds(GROUP + h * HD, HD)],
                (((1,), (1,)), ((), ())),
                preferred_element_type=jnp.float32,
            )
            for h in heads
        ]
        scores = [s * scale + bias[rows, keys] for s in scores]
        shares = [jnp.exp(s - jnp.max(s, axis=-1, keepdims=True)) for s in scores]
        totals = [jnp.sum(s, axis=-1, keepdims=True) for s in shares]
        summed = [
            jnp.dot(
                s.astype(jnp.bfloat16),
                qkv[keys, pl.ds(2 * GROUP + h * HD, HD)],
                preferred_element_type=jnp.float32,
            )
            for h, s in zip(heads, shares)
        ]
        for h in heads:
            attended = (summed[h] / totals[h]).reshape(4, NX, 8, HD)
            for to_x in range(NX):
                part = attended[:, to_x].reshape(32, HD)
                result[to_x, pl.ds(i * 32, 32), pl.ds(h * HD, HD)] = part.astype(jnp.bfloat16)
    for k, out in enumerate(outs):
        out[...] = result[place_x ^ k]


def project_and_attend(place, span_mask, gathered, pieces):
    arrays = [gathered, *pieces]
    return pl.pallas_call(
        attend_kernel,
        out_shape=[jax.ShapeDtypeStruct((TOKENS // NX, GROUP), jnp.bfloat16)] * NX,
        in_specs=[pl.BlockSpec(memory_space=pltpu.SMEM)] * 2
        + [pl.BlockSpec(memory_space=pl.ANY)] * len(arrays),
        out_specs=[pl.BlockSpec(memory_space=pltpu.VMEM)] * NX,
        scratch_shapes=[
            pltpu.VMEM((D // PART, PART, 3 * GROUP), jnp.bfloat16),
            pltpu.VMEM((TOKENS, D), jnp.bfloat16),
            pltpu.VMEM((TOKENS, 3 * GROUP), jnp.float32),
            pltpu.VMEM((TOKENS, 3 * GROUP), jnp.bfloat16),
            pltpu.VMEM((TOKENS, TOKENS), jnp.float32),
            pltpu.VMEM((NX, TOKENS // NX, GROUP), jnp.bfloat16),
            pltpu.SemaphoreType.DMA((D // CHUNK, 3)),
            pltpu.SemaphoreType.DMA((8,)),
        ],
        compiler_params=pltpu.CompilerParams(vmem_limit_bytes=44 * 1024 * 1024),
    )(place, span_mask, *arrays)


def per_device(frames_in, qkv_weight, span_mask):
    z, x, y, c = (lax.axis_index(name) for name in AXES)
    group = x // 2
    hold = lax.optimization_barrier

    places = frames_in.reshape(NZ, NX, 8, D)
    places = lax.dynamic_slice(places, (0, 2 * c, 0, 2 * GROUP * y), (NZ, 2, 8, 2 * GROUP))
    low, high = places[..., :GROUP], places[..., GROUP:]
    low = jnp.where(c == 0, low, low[:, ::-1])
    high = jnp.where(c == 0, high[:, ::-1], high)
    packed = jnp.concatenate([low, high], axis=1).reshape(NZ * NX, 8, GROUP)

    piece = jnp.transpose(qkv_weight, (1, 0, 2))
    first = permute(piece, home)
    other = permute(piece, second)
    slot = jnp.where(c == group, x, 3 - x)
    half = jnp.where(
        slot % 2 == 0,
        jnp.concatenate([first, other], axis=1),
        jnp.concatenate([other, first], axis=1),
    )
    half, packed = hold((half, packed))
    gathered = lax.all_gather(half[None], ("z", "c"), axis=0, tiled=True)
    spread = lax.all_to_all(packed, ("z", "x"), split_axis=0, concat_axis=0, tiled=True)
    spread = spread.reshape(TOKENS, GROUP)
    partner = permute(spread, lambda z, x, y, c: (z, 3 - x, y, c))
    pieces = [spread, partner]
    for shift in SHIFTS[1:]:
        for block in (spread, partner):
            pieces.append(permute(block, lambda z, x, y, c, k=shift: (z, x, y - k, c)))

    place = jnp.stack([y, group, slot]).astype(jnp.int32)
    parts = project_and_attend(place, span_mask, gathered, pieces)
    parts = [permute(part, functools.partial(home, k=k)) for k, part in enumerate(parts)]
    parts = [lax.select_n(x, *[parts[k ^ at] for k in range(NX)]) for at in range(NX)]
    output = jnp.stack([part.reshape(NZ, 8, GROUP) for part in parts], axis=1)
    output = lax.all_to_all(output, "z", split_axis=0, concat_axis=0, tiled=True)
    return output.reshape(1, NZ * NX * 8, GROUP)


def solution(mesh):
    fine = Mesh(mesh.devices.reshape(NZ, NX, NY, NC), AXES)
    in_specs = (P(("z", "x"), None, None), P(("z", "x"), None, ("y", "c")), P())
    out_specs = P(("z", "x"), None, ("y", "c"))
    return jax.shard_map(
        per_device, mesh=fine, in_specs=in_specs, out_specs=out_specs, check_vma=False
    )
```

```python
import jax
import jax.numpy as jnp
from jax import lax
from jax.experimental import pallas as pl
from jax.experimental.pallas import tpu as pltpu
from jax.sharding import Mesh
from jax.sharding import PartitionSpec as P

D = 3072
HD = 128
FRAMES = 64
SPANS = 8
GROUP = 384
NZ, NX, NY, NC = 16, 4, 4, 2
AXES = ("z", "x", "y", "c")
SLICE = D // (NZ * NX)
PART = 2 * SLICE
CHUNK = D // 4
SHIFTS = (0, 1, 3, 2)
TOKENS = FRAMES * 8


def permute(array, where_to):
    pairs = []
    for z in range(NZ):
        for x in range(NX):
            for y in range(NY):
                for c in range(NC):
                    a, b, d, e = where_to(z, x, y, c)
                    source = ((z * NX + x) * NY + y) * NC + c
                    pairs.append((source, (((a % NZ) * NX + b % NX) * NY + d % NY) * NC + e))
    return lax.ppermute(array, AXES, pairs)


def home(z, x, y, c):
    return (z, x if c == x // 2 else 3 - x, y, x // 2)


def second(z, x, y, c):
    near = x ^ 1
    return (z, near if x // 2 == c else 3 - near, y, x // 2)


def attend_kernel(place, mask, gathered, *refs):
    pieces, out = refs[:8], refs[8]
    weights, tokens, sums, qkv, bias, w_sems, x_sems = refs[9:]
    y, group = place[0], place[1]

    token_copies = []
    for i, piece in enumerate(pieces):
        source = lax.rem(y + SHIFTS[i // 2], NY)
        half = group if i % 2 == 0 else 1 - group
        at = pl.multiple_of((2 * source + half) * GROUP, GROUP)
        token_copies.append(pltpu.make_async_copy(piece, tokens.at[:, pl.ds(at, GROUP)], x_sems.at[i]))
    weight_copies = []
    for chunk in range(D // CHUNK):
        parts = pl.ds(chunk * (CHUNK // PART), CHUNK // PART)
        for j in range(3):
            lanes = pl.ds(j * GROUP, GROUP)
            weight_copies.append(
                pltpu.make_async_copy(
                    gathered.at[parts, j], weights.at[parts, :, lanes], w_sems.at[chunk, j]
                )
            )
    for copy in token_copies + weight_copies:
        copy.start()

    span_rows = TOKENS // SPANS
    column = lax.broadcasted_iota(jnp.int32, (1, TOKENS), 1)
    same = (
        lax.broadcasted_iota(jnp.int32, (span_rows, TOKENS), 0) & 7
    ) == (lax.broadcasted_iota(jnp.int32, (span_rows, TOKENS), 1) & 7)
    for i in range(SPANS):
        row = jnp.zeros((1, TOKENS), jnp.int32)
        for j in range(SPANS):
            row = jnp.where((column // span_rows) == j, mask[i, j], row)
        ok = same & (jnp.broadcast_to(row, (span_rows, TOKENS)) > 0)
        bias[pl.ds(i * span_rows, span_rows), :] = jnp.where(ok, 0.0, -1e30)

    for copy in token_copies:
        copy.wait()
    for chunk in range(D // CHUNK):
        for copy in weight_copies[3 * chunk : 3 * chunk + 3]:
            copy.wait()
        features = pl.ds(chunk * CHUNK, CHUNK)
        parts = pl.ds(chunk * (CHUNK // PART), CHUNK // PART)
        product = jnp.dot(
            tokens[:, features],
            weights[parts].reshape(CHUNK, 3 * GROUP),
            preferred_element_type=jnp.float32,
        )
        if chunk:
            product = sums[...] + product
        if chunk < D // CHUNK - 1:
            sums[...] = product
        else:
            qkv[...] = product.astype(jnp.bfloat16)

    scale = 1.0 / jnp.sqrt(jnp.float32(HD))
    heads = range(GROUP // HD)
    for i in range(4):
        rows = pl.ds(i * 128, 128)
        keys = pl.ds(0, (i + 1) * 128)
        scores = [
            lax.dot_general(
                qkv[rows, pl.ds(h * HD, HD)],
                qkv[keys, pl.ds(GROUP + h * HD, HD)],
                (((1,), (1,)), ((), ())),
                preferred_element_type=jnp.float32,
            )
            for h in heads
        ]
        scores = [s * scale + bias[rows, keys] for s in scores]
        shares = [jnp.exp(s - jnp.max(s, axis=-1, keepdims=True)) for s in scores]
        totals = [jnp.sum(s, axis=-1, keepdims=True) for s in shares]
        summed = [
            jnp.dot(
                s.astype(jnp.bfloat16),
                qkv[keys, pl.ds(2 * GROUP + h * HD, HD)],
                preferred_element_type=jnp.float32,
            )
            for h, s in zip(heads, shares)
        ]
        for h in heads:
            attended = (summed[h] / totals[h]).reshape(4, NX, 8, HD)
            for to_x in range(NX):
                part = attended[:, to_x].reshape(32, HD).astype(jnp.bfloat16)
                for core in range(NC):
                    out[NC * to_x + core, pl.ds(i * 32, 32), pl.ds(h * HD, HD)] = part


def project_and_attend(place, span_mask, gathered, pieces):
    arrays = [gathered, *pieces]
    return pl.pallas_call(
        attend_kernel,
        out_shape=jax.ShapeDtypeStruct((NX * NC, TOKENS // NX, GROUP), jnp.bfloat16),
        in_specs=[pl.BlockSpec(memory_space=pltpu.SMEM)] * 2
        + [pl.BlockSpec(memory_space=pl.ANY)] * len(arrays),
        out_specs=pl.BlockSpec(memory_space=pltpu.VMEM),
        scratch_shapes=[
            pltpu.VMEM((D // PART, PART, 3 * GROUP), jnp.bfloat16),
            pltpu.VMEM((TOKENS, D), jnp.bfloat16),
            pltpu.VMEM((TOKENS, 3 * GROUP), jnp.float32),
            pltpu.VMEM((TOKENS, 3 * GROUP), jnp.bfloat16),
            pltpu.VMEM((TOKENS, TOKENS), jnp.float32),
            pltpu.SemaphoreType.DMA((D // CHUNK, 3)),
            pltpu.SemaphoreType.DMA((8,)),
        ],
        compiler_params=pltpu.CompilerParams(vmem_limit_bytes=44 * 1024 * 1024),
    )(place, span_mask, *arrays)


def per_device(frames_in, qkv_weight, span_mask):
    z, x, y, c = (lax.axis_index(name) for name in AXES)
    group = x // 2
    hold = lax.optimization_barrier

    places = frames_in.reshape(NZ, NX, 8, D)
    places = lax.dynamic_slice(places, (0, 2 * c, 0, 2 * GROUP * y), (NZ, 2, 8, 2 * GROUP))
    low, high = places[..., :GROUP], places[..., GROUP:]
    low = jnp.where(c == 0, low, low[:, ::-1])
    high = jnp.where(c == 0, high[:, ::-1], high)
    packed = jnp.concatenate([low, high], axis=1).reshape(NZ * NX, 8, GROUP)

    piece = jnp.transpose(qkv_weight, (1, 0, 2))
    first = permute(piece, home)
    other = permute(piece, second)
    slot = jnp.where(c == group, x, 3 - x)
    half = jnp.where(
        slot % 2 == 0,
        jnp.concatenate([first, other], axis=1),
        jnp.concatenate([other, first], axis=1),
    )
    half, packed = hold((half, packed))
    gathered = lax.all_gather(half[None], ("z", "c"), axis=0, tiled=True)
    spread = lax.all_to_all(packed, ("z", "x"), split_axis=0, concat_axis=0, tiled=True)
    spread = spread.reshape(TOKENS, GROUP)
    partner = permute(spread, lambda z, x, y, c: (z, 3 - x, y, c))
    pieces = [spread, partner]
    for shift in SHIFTS[1:]:
        for block in (spread, partner):
            pieces.append(permute(block, lambda z, x, y, c, k=shift: (z, x, y - k, c)))

    place = jnp.stack([y, group]).astype(jnp.int32)
    output = project_and_attend(place, span_mask, gathered, pieces)
    output = lax.all_to_all(output, ("x", "c"), split_axis=0, concat_axis=0, tiled=True)
    order = ((0, 6), (2, 4), (3, 5), (1, 7))
    parts = [jnp.where(c == 0, output[low], output[high]) for low, high in order]
    output = jnp.stack([part.reshape(NZ, 8, GROUP) for part in parts], axis=1)
    output = lax.all_to_all(output, "z", split_axis=0, concat_axis=0, tiled=True)
    return output.reshape(1, NZ * NX * 8, GROUP)


def solution(mesh):
    fine = Mesh(mesh.devices.reshape(NZ, NX, NY, NC), AXES)
    in_specs = (P(("z", "x"), None, None), P(("z", "x"), None, ("y", "c")), P())
    out_specs = P(("z", "x"), None, ("y", "c"))
    return jax.shard_map(
        per_device, mesh=fine, in_specs=in_specs, out_specs=out_specs, check_vma=False
    )
```

```python
import functools

import jax
import jax.numpy as jnp
from jax import lax
from jax.experimental import pallas as pl
from jax.experimental.pallas import tpu as pltpu
from jax.sharding import Mesh
from jax.sharding import PartitionSpec as P

D = 3072
HD = 128
FRAMES = 64
SPANS = 8
GROUP = 384
NZ, NX, NY, NC = 16, 4, 4, 2
AXES = ("z", "x", "y", "c")
SLICE = D // (NZ * NX)
PART = 2 * SLICE
CHUNK = D // 4
SHIFTS = (0, 1, 3, 2)
TOKENS = FRAMES * 8


def permute(array, where_to):
    pairs = []
    for z in range(NZ):
        for x in range(NX):
            for y in range(NY):
                for c in range(NC):
                    a, b, d, e = where_to(z, x, y, c)
                    source = ((z * NX + x) * NY + y) * NC + c
                    pairs.append((source, (((a % NZ) * NX + b % NX) * NY + d % NY) * NC + e))
    return lax.ppermute(array, AXES, pairs)


def home(z, x, y, c, k=0):
    return (z, (x if c == x // 2 else 3 - x) ^ k, y, x // 2)


def second(z, x, y, c):
    near = x ^ 1
    return (z, near if x // 2 == c else 3 - near, y, x // 2)


def attend_kernel(place, mask, gathered, *refs):
    pieces, out = refs[:8], refs[8]
    weights, tokens, sums, qkv, bias, w_sems, x_sems = refs[9:]
    y, group = place[0], place[1]

    token_copies = []
    for i, piece in enumerate(pieces):
        source = lax.rem(y + SHIFTS[i // 2], NY)
        half = group if i % 2 == 0 else 1 - group
        at = pl.multiple_of((2 * source + half) * GROUP, GROUP)
        token_copies.append(pltpu.make_async_copy(piece, tokens.at[:, pl.ds(at, GROUP)], x_sems.at[i]))
    weight_copies = []
    for chunk in range(D // CHUNK):
        parts = pl.ds(chunk * (CHUNK // PART), CHUNK // PART)
        for j in range(3):
            lanes = pl.ds(j * GROUP, GROUP)
            weight_copies.append(
                pltpu.make_async_copy(
                    gathered.at[parts, j], weights.at[parts, :, lanes], w_sems.at[chunk, j]
                )
            )
    for copy in token_copies + weight_copies:
        copy.start()

    span_rows = TOKENS // SPANS
    column = lax.broadcasted_iota(jnp.int32, (1, TOKENS), 1)
    same = (
        lax.broadcasted_iota(jnp.int32, (span_rows, TOKENS), 0) & 7
    ) == (lax.broadcasted_iota(jnp.int32, (span_rows, TOKENS), 1) & 7)
    for i in range(SPANS):
        row = jnp.zeros((1, TOKENS), jnp.int32)
        for j in range(SPANS):
            row = jnp.where((column // span_rows) == j, mask[i, j], row)
        ok = same & (jnp.broadcast_to(row, (span_rows, TOKENS)) > 0)
        bias[pl.ds(i * span_rows, span_rows), :] = jnp.where(ok, 0.0, -1e30)

    for copy in token_copies:
        copy.wait()
    for chunk in range(D // CHUNK):
        for copy in weight_copies[3 * chunk : 3 * chunk + 3]:
            copy.wait()
        features = pl.ds(chunk * CHUNK, CHUNK)
        parts = pl.ds(chunk * (CHUNK // PART), CHUNK // PART)
        product = jnp.dot(
            tokens[:, features],
            weights[parts].reshape(CHUNK, 3 * GROUP),
            preferred_element_type=jnp.float32,
        )
        if chunk:
            product = sums[...] + product
        if chunk < D // CHUNK - 1:
            sums[...] = product
        else:
            qkv[...] = product.astype(jnp.bfloat16)

    scale = 1.0 / jnp.sqrt(jnp.float32(HD))
    heads = range(GROUP // HD)
    for i in range(4):
        rows = pl.ds(i * 128, 128)
        keys = pl.ds(0, (i + 1) * 128)
        scores = [
            lax.dot_general(
                qkv[rows, pl.ds(h * HD, HD)],
                qkv[keys, pl.ds(GROUP + h * HD, HD)],
                (((1,), (1,)), ((), ())),
                preferred_element_type=jnp.float32,
            )
            for h in heads
        ]
        scores = [s * scale + bias[rows, keys] for s in scores]
        shares = [jnp.exp(s - jnp.max(s, axis=-1, keepdims=True)) for s in scores]
        totals = [jnp.sum(s, axis=-1, keepdims=True) for s in shares]
        summed = [
            jnp.dot(
                s.astype(jnp.bfloat16),
                qkv[keys, pl.ds(2 * GROUP + h * HD, HD)],
                preferred_element_type=jnp.float32,
            )
            for h, s in zip(heads, shares)
        ]
        for h in heads:
            out[rows, pl.ds(h * HD, HD)] = (summed[h] / totals[h]).astype(jnp.bfloat16)


def project_and_attend(place, span_mask, gathered, pieces):
    arrays = [gathered, *pieces]
    return pl.pallas_call(
        attend_kernel,
        out_shape=jax.ShapeDtypeStruct((TOKENS, GROUP), jnp.bfloat16),
        in_specs=[pl.BlockSpec(memory_space=pltpu.SMEM)] * 2
        + [pl.BlockSpec(memory_space=pl.ANY)] * len(arrays),
        out_specs=pl.BlockSpec(memory_space=pltpu.VMEM),
        scratch_shapes=[
            pltpu.VMEM((D // PART, PART, 3 * GROUP), jnp.bfloat16),
            pltpu.VMEM((TOKENS, D), jnp.bfloat16),
            pltpu.VMEM((TOKENS, 3 * GROUP), jnp.float32),
            pltpu.VMEM((TOKENS, 3 * GROUP), jnp.bfloat16),
            pltpu.VMEM((TOKENS, TOKENS), jnp.float32),
            pltpu.SemaphoreType.DMA((D // CHUNK, 3)),
            pltpu.SemaphoreType.DMA((8,)),
        ],
        compiler_params=pltpu.CompilerParams(vmem_limit_bytes=44 * 1024 * 1024),
    )(place, span_mask, *arrays)


def per_device(frames_in, qkv_weight, span_mask):
    z, x, y, c = (lax.axis_index(name) for name in AXES)
    group = x // 2
    hold = lax.optimization_barrier

    places = frames_in.reshape(NZ, NX, 8, D)
    places = lax.dynamic_slice(places, (0, 2 * c, 0, 2 * GROUP * y), (NZ, 2, 8, 2 * GROUP))
    low, high = places[..., :GROUP], places[..., GROUP:]
    low = jnp.where(c == 0, low, low[:, ::-1])
    high = jnp.where(c == 0, high[:, ::-1], high)
    packed = jnp.concatenate([low, high], axis=1).reshape(NZ * NX, 8, GROUP)

    piece = jnp.transpose(qkv_weight, (1, 0, 2))
    first = permute(piece, home)
    other = permute(piece, second)
    slot = jnp.where(c == group, x, 3 - x)
    half = jnp.where(
        slot % 2 == 0,
        jnp.concatenate([first, other], axis=1),
        jnp.concatenate([other, first], axis=1),
    )
    half, packed = hold((half, packed))
    gathered = lax.all_gather(half[None], ("z", "c"), axis=0, tiled=True)
    spread = lax.all_to_all(packed, ("z", "x"), split_axis=0, concat_axis=0, tiled=True)
    spread = spread.reshape(TOKENS, GROUP)
    partner = permute(spread, lambda z, x, y, c: (z, 3 - x, y, c))
    pieces = [spread, partner]
    for shift in SHIFTS[1:]:
        for block in (spread, partner):
            pieces.append(permute(block, lambda z, x, y, c, k=shift: (z, x, y - k, c)))

    place = jnp.stack([y, group]).astype(jnp.int32)
    output = project_and_attend(place, span_mask, gathered, pieces)
    output = output.reshape(NZ, NX, 8, GROUP)
    output = lax.all_to_all(output, "z", split_axis=0, concat_axis=0, tiled=True)
    parts = []
    for k in range(NX):
        part = lax.dynamic_index_in_dim(output, slot ^ k, axis=1, keepdims=False)
        parts.append(permute(part, functools.partial(home, k=k)))
    parts = [lax.select_n(x, *[parts[k ^ at] for k in range(NX)]) for at in range(NX)]
    return jnp.stack(parts, axis=1).reshape(1, NZ * NX * 8, GROUP)


def solution(mesh):
    fine = Mesh(mesh.devices.reshape(NZ, NX, NY, NC), AXES)
    in_specs = (P(("z", "x"), None, None), P(("z", "x"), None, ("y", "c")), P())
    out_specs = P(("z", "x"), None, ("y", "c"))
    return jax.shard_map(
        per_device, mesh=fine, in_specs=in_specs, out_specs=out_specs, check_vma=False
    )
```

```python
import functools

import jax
import jax.numpy as jnp
from jax import lax
from jax.experimental import pallas as pl
from jax.experimental.pallas import tpu as pltpu
from jax.sharding import Mesh
from jax.sharding import PartitionSpec as P

D = 3072
HD = 128
FRAMES = 64
SPANS = 8
GROUP = 384
NZ, NX, NY, NC = 16, 4, 4, 2
AXES = ("z", "x", "y", "c")
SLICE = D // (NZ * NX)
PART = 2 * SLICE
CHUNK = D // 4
BLOCK = GROUP // PART
SHIFTS = (0, 1, 3, 2)
TOKENS = FRAMES * 8


def permute(array, where_to):
    pairs = []
    for z in range(NZ):
        for x in range(NX):
            for y in range(NY):
                for c in range(NC):
                    a, b, d, e = where_to(z, x, y, c)
                    source = ((z * NX + x) * NY + y) * NC + c
                    pairs.append((source, (((a % NZ) * NX + b % NX) * NY + d % NY) * NC + e))
    return lax.ppermute(array, AXES, pairs)


def home(z, x, y, c, k=0):
    return (z, (x if c == x // 2 else 3 - x) ^ k, y, x // 2)


def second(z, x, y, c):
    near = x ^ 1
    return (z, near if x // 2 == c else 3 - near, y, x // 2)


def attend_kernel(place, mask, gathered, *refs):
    pieces, outs = refs[:8], refs[8:12]
    weights, sums, qkv, bias, result, w_sems = refs[12:]
    y, group, place_x = place[0], place[1], place[2]

    weight_copies = []
    for i in range(8):
        half = group if i % 2 == 0 else 1 - group
        source = (2 * lax.rem(y + SHIFTS[i // 2], NY) + half) * BLOCK
        for j in range(3):
            lanes = pl.ds(j * GROUP, GROUP)
            weight_copies.append(
                pltpu.make_async_copy(
                    gathered.at[pl.ds(source, BLOCK), j],
                    weights.at[pl.ds(i * BLOCK, BLOCK), :, lanes],
                    w_sems.at[i, j],
                )
            )
    for copy in weight_copies:
        copy.start()

    span_rows = TOKENS // SPANS
    column = lax.broadcasted_iota(jnp.int32, (1, TOKENS), 1)
    same = (
        lax.broadcasted_iota(jnp.int32, (span_rows, TOKENS), 0) & 7
    ) == (lax.broadcasted_iota(jnp.int32, (span_rows, TOKENS), 1) & 7)
    for i in range(SPANS):
        row = jnp.zeros((1, TOKENS), jnp.int32)
        for j in range(SPANS):
            row = jnp.where((column // span_rows) == j, mask[i, j], row)
        ok = same & (jnp.broadcast_to(row, (span_rows, TOKENS)) > 0)
        bias[pl.ds(i * span_rows, span_rows), :] = jnp.where(ok, 0.0, -1e30)

    for chunk in range(D // CHUNK):
        for copy in weight_copies[6 * chunk : 6 * chunk + 6]:
            copy.wait()
        parts = pl.ds(chunk * (CHUNK // PART), CHUNK // PART)
        product = jnp.dot(
            jnp.concatenate([pieces[2 * chunk][...], pieces[2 * chunk + 1][...]], axis=1),
            weights[parts].reshape(CHUNK, 3 * GROUP),
            preferred_element_type=jnp.float32,
        )
        if chunk:
            product = sums[...] + product
        if chunk < D // CHUNK - 1:
            sums[...] = product
        else:
            qkv[...] = product.astype(jnp.bfloat16)

    scale = 1.0 / jnp.sqrt(jnp.float32(HD))
    heads = range(GROUP // HD)
    for i in range(4):
        rows = pl.ds(i * 128, 128)
        keys = pl.ds(0, (i + 1) * 128)
        scores = [
            lax.dot_general(
                qkv[rows, pl.ds(h * HD, HD)],
                qkv[keys, pl.ds(GROUP + h * HD, HD)],
                (((1,), (1,)), ((), ())),
                preferred_element_type=jnp.float32,
            )
            for h in heads
        ]
        scores = [s * scale + bias[rows, keys] for s in scores]
        shares = [jnp.exp(s - jnp.max(s, axis=-1, keepdims=True)) for s in scores]
        totals = [jnp.sum(s, axis=-1, keepdims=True) for s in shares]
        summed = [
            jnp.dot(
                s.astype(jnp.bfloat16),
                qkv[keys, pl.ds(2 * GROUP + h * HD, HD)],
                preferred_element_type=jnp.float32,
            )
            for h, s in zip(heads, shares)
        ]
        for h in heads:
            attended = (summed[h] / totals[h]).reshape(4, NX, 8, HD)
            for to_x in range(NX):
                part = attended[:, to_x].reshape(32, HD)
                result[to_x, pl.ds(i * 32, 32), pl.ds(h * HD, HD)] = part.astype(jnp.bfloat16)
    for k, out in enumerate(outs):
        out[...] = result[place_x ^ k]


def project_and_attend(place, span_mask, gathered, pieces):
    arrays = [gathered, *pieces]
    return pl.pallas_call(
        attend_kernel,
        out_shape=[jax.ShapeDtypeStruct((TOKENS // NX, GROUP), jnp.bfloat16)] * NX,
        in_specs=[pl.BlockSpec(memory_space=pltpu.SMEM)] * 2
        + [pl.BlockSpec(memory_space=pl.ANY)]
        + [pl.BlockSpec(memory_space=pltpu.VMEM)] * len(pieces),
        out_specs=[pl.BlockSpec(memory_space=pltpu.VMEM)] * NX,
        scratch_shapes=[
            pltpu.VMEM((D // PART, PART, 3 * GROUP), jnp.bfloat16),
            pltpu.VMEM((TOKENS, 3 * GROUP), jnp.float32),
            pltpu.VMEM((TOKENS, 3 * GROUP), jnp.bfloat16),
            pltpu.VMEM((TOKENS, TOKENS), jnp.float32),
            pltpu.VMEM((NX, TOKENS // NX, GROUP), jnp.bfloat16),
            pltpu.SemaphoreType.DMA((8, 3)),
        ],
        compiler_params=pltpu.CompilerParams(vmem_limit_bytes=40 * 1024 * 1024),
    )(place, span_mask, *arrays)


def per_device(frames_in, qkv_weight, span_mask):
    z, x, y, c = (lax.axis_index(name) for name in AXES)
    group = x // 2
    hold = lax.optimization_barrier

    places = frames_in.reshape(NZ, NX, 8, D)
    places = lax.dynamic_slice(places, (0, 2 * c, 0, 2 * GROUP * y), (NZ, 2, 8, 2 * GROUP))
    low, high = places[..., :GROUP], places[..., GROUP:]
    low = jnp.where(c == 0, low, low[:, ::-1])
    high = jnp.where(c == 0, high[:, ::-1], high)
    packed = jnp.concatenate([low, high], axis=1).reshape(NZ * NX, 8, GROUP)

    piece = jnp.transpose(qkv_weight, (1, 0, 2))
    first = permute(piece, home)
    other = permute(piece, second)
    slot = jnp.where(c == group, x, 3 - x)
    half = jnp.where(
        slot % 2 == 0,
        jnp.concatenate([first, other], axis=1),
        jnp.concatenate([other, first], axis=1),
    )
    half, packed = hold((half, packed))
    gathered = lax.all_gather(half[None], ("z", "c"), axis=0, tiled=True)
    spread = lax.all_to_all(packed, ("z", "x"), split_axis=0, concat_axis=0, tiled=True)
    spread = spread.reshape(TOKENS, GROUP)
    partner = permute(spread, lambda z, x, y, c: (z, 3 - x, y, c))
    pieces = [spread, partner]
    for shift in SHIFTS[1:]:
        for block in (spread, partner):
            pieces.append(permute(block, lambda z, x, y, c, k=shift: (z, x, y - k, c)))

    place = jnp.stack([y, group, slot]).astype(jnp.int32)
    parts = project_and_attend(place, span_mask, gathered, pieces)
    parts = [permute(part, functools.partial(home, k=k)) for k, part in enumerate(parts)]
    parts = [lax.select_n(x, *[parts[k ^ at] for k in range(NX)]) for at in range(NX)]
    output = jnp.stack([part.reshape(NZ, 8, GROUP) for part in parts], axis=1)
    output = lax.all_to_all(output, "z", split_axis=0, concat_axis=0, tiled=True)
    return output.reshape(1, NZ * NX * 8, GROUP)


def solution(mesh):
    fine = Mesh(mesh.devices.reshape(NZ, NX, NY, NC), AXES)
    in_specs = (P(("z", "x"), None, None), P(("z", "x"), None, ("y", "c")), P())
    out_specs = P(("z", "x"), None, ("y", "c"))
    return jax.shard_map(
        per_device, mesh=fine, in_specs=in_specs, out_specs=out_specs, check_vma=False
    )
```

```python
import functools

import jax
import jax.numpy as jnp
from jax import lax
from jax.experimental import pallas as pl
from jax.experimental.pallas import tpu as pltpu
from jax.sharding import Mesh
from jax.sharding import PartitionSpec as P

D = 3072
HD = 128
FRAMES = 64
SPANS = 8
GROUP = 384
NZ, NX, NY, NC = 16, 4, 4, 2
AXES = ("z", "x", "y", "c")
SLICE = D // (NZ * NX)
PART = 2 * SLICE
CHUNK = D // 4
BLOCK = GROUP // PART
SHIFTS = (0, 1, 3, 2)
TOKENS = FRAMES * 8


def permute(array, where_to):
    pairs = []
    for z in range(NZ):
        for x in range(NX):
            for y in range(NY):
                for c in range(NC):
                    a, b, d, e = where_to(z, x, y, c)
                    source = ((z * NX + x) * NY + y) * NC + c
                    pairs.append((source, (((a % NZ) * NX + b % NX) * NY + d % NY) * NC + e))
    return lax.ppermute(array, AXES, pairs)


def home(z, x, y, c, k=0):
    return (z, (x if c == x // 2 else 3 - x) ^ k, y, x // 2)


def second(z, x, y, c):
    near = x ^ 1
    return (z, near if x // 2 == c else 3 - near, y, x // 2)


def attend_kernel(place, mask, gathered, *refs):
    pieces, outs = refs[:8], refs[8:12]
    weights, sums, qkv, bias, result, w_sems = refs[12:]
    y, group, place_x = place[0], place[1], place[2]

    weight_copies = []
    for i in range(8):
        half = group if i % 2 == 0 else 1 - group
        source = (2 * lax.rem(y + SHIFTS[i // 2], NY) + half) * BLOCK
        for j in range(3):
            lanes = pl.ds(j * GROUP, GROUP)
            weight_copies.append(
                pltpu.make_async_copy(
                    gathered.at[pl.ds(source, BLOCK), j],
                    weights.at[pl.ds(i * BLOCK, BLOCK), :, lanes],
                    w_sems.at[i, j],
                )
            )
    for copy in weight_copies:
        copy.start()

    span_rows = TOKENS // SPANS
    column = lax.broadcasted_iota(jnp.int32, (1, TOKENS), 1)
    same = (
        lax.broadcasted_iota(jnp.int32, (span_rows, TOKENS), 0) & 7
    ) == (lax.broadcasted_iota(jnp.int32, (span_rows, TOKENS), 1) & 7)
    for i in range(SPANS):
        row = jnp.zeros((1, TOKENS), jnp.int32)
        for j in range(SPANS):
            row = jnp.where((column // span_rows) == j, mask[i, j], row)
        ok = same & (jnp.broadcast_to(row, (span_rows, TOKENS)) > 0)
        bias[pl.ds(i * span_rows, span_rows), :] = jnp.where(ok, 0.0, -1e30)

    for chunk in range(D // CHUNK):
        for copy in weight_copies[6 * chunk : 6 * chunk + 6]:
            copy.wait()
        parts = pl.ds(chunk * (CHUNK // PART), CHUNK // PART)
        product = jnp.dot(
            jnp.concatenate([pieces[2 * chunk][...], pieces[2 * chunk + 1][...]], axis=1),
            weights[parts].reshape(CHUNK, 3 * GROUP),
            preferred_element_type=jnp.float32,
        )
        if chunk:
            product = sums[...] + product
        if chunk < D // CHUNK - 1:
            sums[...] = product
        else:
            qkv[...] = product.astype(jnp.bfloat16)

    scale = 1.0 / jnp.sqrt(jnp.float32(HD))
    heads = range(GROUP // HD)
    for i in range(4):
        rows = pl.ds(i * 128, 128)
        keys = pl.ds(0, (i + 1) * 128)
        scores = [
            lax.dot_general(
                qkv[rows, pl.ds(h * HD, HD)],
                qkv[keys, pl.ds(GROUP + h * HD, HD)],
                (((1,), (1,)), ((), ())),
                preferred_element_type=jnp.float32,
            )
            for h in heads
        ]
        scores = [s * scale + bias[rows, keys] for s in scores]
        shares = [jnp.exp(s - jnp.max(s, axis=-1, keepdims=True)) for s in scores]
        totals = [jnp.sum(s, axis=-1, keepdims=True) for s in shares]
        summed = [
            jnp.dot(
                s.astype(jnp.bfloat16),
                qkv[keys, pl.ds(2 * GROUP + h * HD, HD)],
                preferred_element_type=jnp.float32,
            )
            for h, s in zip(heads, shares)
        ]
        for h in heads:
            attended = (summed[h] / totals[h]).reshape(4, NX, 8, HD)
            for to_x in range(NX):
                part = attended[:, to_x].reshape(32, HD)
                result[to_x, pl.ds(i * 32, 32), pl.ds(h * HD, HD)] = part.astype(jnp.bfloat16)
    for k, out in enumerate(outs):
        out[...] = result[place_x ^ k]


def project_and_attend(place, span_mask, gathered, pieces):
    arrays = [gathered, *pieces]
    return pl.pallas_call(
        attend_kernel,
        out_shape=[jax.ShapeDtypeStruct((TOKENS // NX, GROUP), jnp.bfloat16)] * NX,
        in_specs=[pl.BlockSpec(memory_space=pltpu.SMEM)] * 2
        + [pl.BlockSpec(memory_space=pl.ANY)]
        + [pl.BlockSpec(memory_space=pltpu.VMEM)] * len(pieces),
        out_specs=[pl.BlockSpec(memory_space=pltpu.VMEM)] * NX,
        scratch_shapes=[
            pltpu.VMEM((D // PART, PART, 3 * GROUP), jnp.bfloat16),
            pltpu.VMEM((TOKENS, 3 * GROUP), jnp.float32),
            pltpu.VMEM((TOKENS, 3 * GROUP), jnp.bfloat16),
            pltpu.VMEM((TOKENS, TOKENS), jnp.float32),
            pltpu.VMEM((NX, TOKENS // NX, GROUP), jnp.bfloat16),
            pltpu.SemaphoreType.DMA((8, 3)),
        ],
        compiler_params=pltpu.CompilerParams(vmem_limit_bytes=54 * 1024 * 1024),
    )(place, span_mask, *arrays)


def per_device(frames_in, qkv_weight, span_mask):
    z, x, y, c = (lax.axis_index(name) for name in AXES)
    group = x // 2
    hold = lax.optimization_barrier

    places = frames_in.reshape(NZ, NX, 8, D)
    places = lax.dynamic_slice(places, (0, 2 * c, 0, 2 * GROUP * y), (NZ, 2, 8, 2 * GROUP))
    low, high = places[..., :GROUP], places[..., GROUP:]
    low = jnp.where(c == 0, low, low[:, ::-1])
    high = jnp.where(c == 0, high[:, ::-1], high)
    packed = jnp.concatenate([low, high], axis=1).reshape(NZ * NX, 8, GROUP)

    piece = jnp.transpose(qkv_weight, (1, 0, 2))
    first = permute(piece, home)
    other = permute(piece, second)
    slot = jnp.where(c == group, x, 3 - x)
    half = jnp.where(
        slot % 2 == 0,
        jnp.concatenate([first, other], axis=1),
        jnp.concatenate([other, first], axis=1),
    )
    half, packed = hold((half, packed))
    gathered = lax.all_gather(half[None], ("z", "c"), axis=0, tiled=True)
    spread = lax.all_to_all(packed, ("z", "x"), split_axis=0, concat_axis=0, tiled=True)
    spread = spread.reshape(TOKENS, GROUP)
    partner = permute(spread, lambda z, x, y, c: (z, 3 - x, y, c))
    pieces = [spread, partner]
    for shift in SHIFTS[1:]:
        for block in (spread, partner):
            pieces.append(permute(block, lambda z, x, y, c, k=shift: (z, x, y - k, c)))

    place = jnp.stack([y, group, slot]).astype(jnp.int32)
    parts = project_and_attend(place, span_mask, gathered, pieces)
    parts = [permute(part, functools.partial(home, k=k)) for k, part in enumerate(parts)]
    parts = [lax.select_n(x, *[parts[k ^ at] for k in range(NX)]) for at in range(NX)]
    output = jnp.stack([part.reshape(NZ, 8, GROUP) for part in parts], axis=1)
    output = lax.all_to_all(output, "z", split_axis=0, concat_axis=0, tiled=True)
    return output.reshape(1, NZ * NX * 8, GROUP)


def solution(mesh):
    fine = Mesh(mesh.devices.reshape(NZ, NX, NY, NC), AXES)
    in_specs = (P(("z", "x"), None, None), P(("z", "x"), None, ("y", "c")), P())
    out_specs = P(("z", "x"), None, ("y", "c"))
    return jax.shard_map(
        per_device, mesh=fine, in_specs=in_specs, out_specs=out_specs, check_vma=False
    )
```

```python
import functools

import jax
import jax.numpy as jnp
from jax import lax
from jax.experimental import pallas as pl
from jax.experimental.pallas import tpu as pltpu
from jax.sharding import Mesh
from jax.sharding import PartitionSpec as P

D = 3072
HD = 128
FRAMES = 64
SPANS = 8
GROUP = 384
NZ, NX, NY, NC = 16, 4, 4, 2
AXES = ("z", "x", "y", "c")
SLICE = D // (NZ * NX)
PART = 2 * SLICE
CHUNK = D // 4
SHIFTS = (0, 1, 3, 2)
TOKENS = FRAMES * 8


def permute(array, where_to):
    pairs = []
    for z in range(NZ):
        for x in range(NX):
            for y in range(NY):
                for c in range(NC):
                    a, b, d, e = where_to(z, x, y, c)
                    source = ((z * NX + x) * NY + y) * NC + c
                    pairs.append((source, (((a % NZ) * NX + b % NX) * NY + d % NY) * NC + e))
    return lax.ppermute(array, AXES, pairs)


def home(z, x, y, c, k=0):
    return (z, (x if c == x // 2 else 3 - x) ^ k, y, x // 2)


def second(z, x, y, c):
    near = x ^ 1
    return (z, near if x // 2 == c else 3 - near, y, x // 2)


def attend_kernel(place, mask, gathered, *refs):
    pieces, outs = refs[:8], refs[8:12]
    weights, tokens, sums, qkv, bias, result, w_sems, x_sems = refs[12:]
    y, group, place_x = place[0], place[1], place[2]

    token_copies, weight_copies = [], []
    per_chunk = CHUNK // PART
    for i, piece in enumerate(pieces):
        half = group if i % 2 == 0 else 1 - group
        at = pl.multiple_of(i // 2 * CHUNK + half * GROUP, GROUP)
        token_copies.append(pltpu.make_async_copy(piece, tokens.at[:, pl.ds(at, GROUP)], x_sems.at[i]))
    for chunk in range(D // CHUNK):
        source = lax.rem(y + SHIFTS[chunk], NY) * per_chunk
        parts = pl.ds(chunk * per_chunk, per_chunk)
        for j in range(3):
            lanes = pl.ds(j * GROUP, GROUP)
            weight_copies.append(
                pltpu.make_async_copy(
                    gathered.at[pl.ds(source, per_chunk), j],
                    weights.at[parts, :, lanes],
                    w_sems.at[chunk, j],
                )
            )
    for chunk in range(D // CHUNK):
        for copy in token_copies[2 * chunk : 2 * chunk + 2] + weight_copies[3 * chunk : 3 * chunk + 3]:
            copy.start()

    span_rows = TOKENS // SPANS
    column = lax.broadcasted_iota(jnp.int32, (1, TOKENS), 1)
    same = (
        lax.broadcasted_iota(jnp.int32, (span_rows, TOKENS), 0) & 7
    ) == (lax.broadcasted_iota(jnp.int32, (span_rows, TOKENS), 1) & 7)
    for i in range(SPANS):
        row = jnp.zeros((1, TOKENS), jnp.int32)
        for j in range(SPANS):
            row = jnp.where((column // span_rows) == j, mask[i, j], row)
        ok = same & (jnp.broadcast_to(row, (span_rows, TOKENS)) > 0)
        bias[pl.ds(i * span_rows, span_rows), :] = jnp.where(ok, 0.0, -1e30)

    for chunk in range(D // CHUNK):
        for copy in token_copies[2 * chunk : 2 * chunk + 2] + weight_copies[3 * chunk : 3 * chunk + 3]:
            copy.wait()
        features = pl.ds(chunk * CHUNK, CHUNK)
        parts = pl.ds(chunk * (CHUNK // PART), CHUNK // PART)
        product = jnp.dot(
            tokens[:, features],
            weights[parts].reshape(CHUNK, 3 * GROUP),
            preferred_element_type=jnp.float32,
        )
        if chunk:
            product = sums[...] + product
        if chunk < D // CHUNK - 1:
            sums[...] = product
        else:
            qkv[...] = product.astype(jnp.bfloat16)

    scale = 1.0 / jnp.sqrt(jnp.float32(HD))
    heads = range(GROUP // HD)
    for i in range(4):
        rows = pl.ds(i * 128, 128)
        keys = pl.ds(0, (i + 1) * 128)
        scores = [
            lax.dot_general(
                qkv[rows, pl.ds(h * HD, HD)],
                qkv[keys, pl.ds(GROUP + h * HD, HD)],
                (((1,), (1,)), ((), ())),
                preferred_element_type=jnp.float32,
            )
            for h in heads
        ]
        scores = [s * scale + bias[rows, keys] for s in scores]
        shares = [jnp.exp(s - jnp.max(s, axis=-1, keepdims=True)) for s in scores]
        totals = [jnp.sum(s, axis=-1, keepdims=True) for s in shares]
        summed = [
            jnp.dot(
                s.astype(jnp.bfloat16),
                qkv[keys, pl.ds(2 * GROUP + h * HD, HD)],
                preferred_element_type=jnp.float32,
            )
            for h, s in zip(heads, shares)
        ]
        for h in heads:
            attended = (summed[h] / totals[h]).reshape(4, NX, 8, HD)
            for to_x in range(NX):
                part = attended[:, to_x].reshape(32, HD)
                result[to_x, pl.ds(i * 32, 32), pl.ds(h * HD, HD)] = part.astype(jnp.bfloat16)
    for k, out in enumerate(outs):
        out[...] = result[place_x ^ k]


def project_and_attend(place, span_mask, gathered, pieces):
    arrays = [gathered, *pieces]
    return pl.pallas_call(
        attend_kernel,
        out_shape=[jax.ShapeDtypeStruct((TOKENS // NX, GROUP), jnp.bfloat16)] * NX,
        in_specs=[pl.BlockSpec(memory_space=pltpu.SMEM)] * 2
        + [pl.BlockSpec(memory_space=pl.ANY)] * len(arrays),
        out_specs=[pl.BlockSpec(memory_space=pltpu.VMEM)] * NX,
        scratch_shapes=[
            pltpu.VMEM((D // PART, PART, 3 * GROUP), jnp.bfloat16),
            pltpu.VMEM((TOKENS, D), jnp.bfloat16),
            pltpu.VMEM((TOKENS, 3 * GROUP), jnp.float32),
            pltpu.VMEM((TOKENS, 3 * GROUP), jnp.bfloat16),
            pltpu.VMEM((TOKENS, TOKENS), jnp.float32),
            pltpu.VMEM((NX, TOKENS // NX, GROUP), jnp.bfloat16),
            pltpu.SemaphoreType.DMA((D // CHUNK, 3)),
            pltpu.SemaphoreType.DMA((8,)),
        ],
        compiler_params=pltpu.CompilerParams(vmem_limit_bytes=44 * 1024 * 1024),
    )(place, span_mask, *arrays)


def per_device(frames_in, qkv_weight, span_mask):
    z, x, y, c = (lax.axis_index(name) for name in AXES)
    group = x // 2
    hold = lax.optimization_barrier

    places = frames_in.reshape(NZ, NX, 8, D)
    places = lax.dynamic_slice(places, (0, 2 * c, 0, 2 * GROUP * y), (NZ, 2, 8, 2 * GROUP))
    low, high = places[..., :GROUP], places[..., GROUP:]
    low = jnp.where(c == 0, low, low[:, ::-1])
    high = jnp.where(c == 0, high[:, ::-1], high)
    packed = jnp.concatenate([low, high], axis=1).reshape(NZ * NX, 8, GROUP)

    piece = jnp.transpose(qkv_weight, (1, 0, 2))
    first = permute(piece, home)
    other = permute(piece, second)
    slot = jnp.where(c == group, x, 3 - x)
    half = jnp.where(
        slot % 2 == 0,
        jnp.concatenate([first, other], axis=1),
        jnp.concatenate([other, first], axis=1),
    )
    half, packed = hold((half, packed))
    gathered = lax.all_gather(half[None], ("z", "c"), axis=0, tiled=True)
    spread = lax.all_to_all(packed, ("z", "x"), split_axis=0, concat_axis=0, tiled=True)
    spread = spread.reshape(TOKENS, GROUP)
    partner = permute(spread, lambda z, x, y, c: (z, 3 - x, y, c))
    pieces = [spread, partner]
    for shift in SHIFTS[1:]:
        for block in (spread, partner):
            pieces.append(permute(block, lambda z, x, y, c, k=shift: (z, x, y - k, c)))

    place = jnp.stack([y, group, slot]).astype(jnp.int32)
    parts = project_and_attend(place, span_mask, gathered, pieces)
    parts = [permute(part, functools.partial(home, k=k)) for k, part in enumerate(parts)]
    parts = [lax.select_n(x, *[parts[k ^ at] for k in range(NX)]) for at in range(NX)]
    output = jnp.stack([part.reshape(NZ, 8, GROUP) for part in parts], axis=1)
    output = lax.all_to_all(output, "z", split_axis=0, concat_axis=0, tiled=True)
    return output.reshape(1, NZ * NX * 8, GROUP)


def solution(mesh):
    fine = Mesh(mesh.devices.reshape(NZ, NX, NY, NC), AXES)
    in_specs = (P(("z", "x"), None, None), P(("z", "x"), None, ("y", "c")), P())
    out_specs = P(("z", "x"), None, ("y", "c"))
    return jax.shard_map(
        per_device, mesh=fine, in_specs=in_specs, out_specs=out_specs, check_vma=False
    )
```

```python
import functools

import jax
import jax.numpy as jnp
from jax import lax
from jax.experimental import pallas as pl
from jax.experimental.pallas import tpu as pltpu
from jax.sharding import Mesh
from jax.sharding import PartitionSpec as P

D = 3072
HD = 128
FRAMES = 64
SPANS = 8
GROUP = 384
NZ, NX, NY, NC = 16, 4, 4, 2
AXES = ("z", "x", "y", "c")
SLICE = D // (NZ * NX)
PART = 2 * SLICE
CHUNK = D // 4
SHIFTS = (0, 1, 3, 2)
TOKENS = FRAMES * 8


def permute(array, where_to):
    pairs = []
    for z in range(NZ):
        for x in range(NX):
            for y in range(NY):
                for c in range(NC):
                    a, b, d, e = where_to(z, x, y, c)
                    source = ((z * NX + x) * NY + y) * NC + c
                    pairs.append((source, (((a % NZ) * NX + b % NX) * NY + d % NY) * NC + e))
    return lax.ppermute(array, AXES, pairs)


def home(z, x, y, c, k=0):
    return (z, (x if c == x // 2 else 3 - x) ^ k, y, x // 2)


def second(z, x, y, c):
    near = x ^ 1
    return (z, near if x // 2 == c else 3 - near, y, x // 2)


def attend_kernel(place, mask, gathered, *refs):
    pieces, outs = refs[:8], refs[8:12]
    weights, tokens, sums, qkv, bias, result, w_sems, x_sems = refs[12:]
    y, group, place_x = place[0], place[1], place[2]

    token_copies, weight_copies = [], []
    per_chunk = CHUNK // PART
    for i, piece in enumerate(pieces):
        half = group if i % 2 == 0 else 1 - group
        at = pl.multiple_of(i // 2 * CHUNK + half * GROUP, GROUP)
        token_copies.append(pltpu.make_async_copy(piece, tokens.at[:, pl.ds(at, GROUP)], x_sems.at[i]))
    for chunk in range(D // CHUNK):
        source = lax.rem(y + SHIFTS[chunk], NY) * per_chunk
        parts = pl.ds(chunk * per_chunk, per_chunk)
        for j in range(3):
            lanes = pl.ds(j * GROUP, GROUP)
            weight_copies.append(
                pltpu.make_async_copy(
                    gathered.at[pl.ds(source, per_chunk), j],
                    weights.at[parts, :, lanes],
                    w_sems.at[chunk, j],
                )
            )
    for chunk in range(D // CHUNK):
        for copy in token_copies[2 * chunk : 2 * chunk + 2] + weight_copies[3 * chunk : 3 * chunk + 3]:
            copy.start()

    span_rows = TOKENS // SPANS
    column = lax.broadcasted_iota(jnp.int32, (1, TOKENS), 1)
    same = (
        lax.broadcasted_iota(jnp.int32, (span_rows, TOKENS), 0) & 7
    ) == (lax.broadcasted_iota(jnp.int32, (span_rows, TOKENS), 1) & 7)
    for i in range(SPANS):
        row = jnp.zeros((1, TOKENS), jnp.int32)
        for j in range(SPANS):
            row = jnp.where((column // span_rows) == j, mask[i, j], row)
        ok = same & (jnp.broadcast_to(row, (span_rows, TOKENS)) > 0)
        bias[pl.ds(i * span_rows, span_rows), :] = jnp.where(ok, 0.0, -1e30)

    for chunk in range(D // CHUNK):
        for copy in token_copies[2 * chunk : 2 * chunk + 2] + weight_copies[3 * chunk : 3 * chunk + 3]:
            copy.wait()
        features = pl.ds(chunk * CHUNK, CHUNK)
        parts = pl.ds(chunk * (CHUNK // PART), CHUNK // PART)
        product = jnp.dot(
            tokens[:, features],
            weights[parts].reshape(CHUNK, 3 * GROUP),
            preferred_element_type=jnp.float32,
        )
        if chunk:
            product = sums[...] + product
        if chunk < D // CHUNK - 1:
            sums[...] = product
        else:
            qkv[...] = product.astype(jnp.bfloat16)

    scale = 1.0 / jnp.sqrt(jnp.float32(HD))
    heads = range(GROUP // HD)
    for i in range(4):
        rows = pl.ds(i * 128, 128)
        keys = pl.ds(0, (i + 1) * 128)
        scores = [
            lax.dot_general(
                qkv[rows, pl.ds(h * HD, HD)],
                qkv[keys, pl.ds(GROUP + h * HD, HD)],
                (((1,), (1,)), ((), ())),
                preferred_element_type=jnp.float32,
            )
            for h in heads
        ]
        scores = [s * scale + bias[rows, keys] for s in scores]
        shares = [jnp.exp(s - jnp.max(s, axis=-1, keepdims=True)) for s in scores]
        totals = [jnp.sum(s, axis=-1, keepdims=True) for s in shares]
        summed = [
            jnp.dot(
                s.astype(jnp.bfloat16),
                qkv[keys, pl.ds(2 * GROUP + h * HD, HD)],
                preferred_element_type=jnp.float32,
            )
            for h, s in zip(heads, shares)
        ]
        for h in heads:
            attended = (summed[h] / totals[h]).reshape(4, NX, 8, HD)
            for to_x in range(NX):
                part = attended[:, to_x].reshape(32, HD)
                result[to_x, pl.ds(i * 32, 32), pl.ds(h * HD, HD)] = part.astype(jnp.bfloat16)
    for k, out in enumerate(outs):
        out[...] = result[place_x ^ k]


def project_and_attend(place, span_mask, gathered, pieces):
    arrays = [gathered, *pieces]
    return pl.pallas_call(
        attend_kernel,
        out_shape=[jax.ShapeDtypeStruct((TOKENS // NX, GROUP), jnp.bfloat16)] * NX,
        in_specs=[pl.BlockSpec(memory_space=pltpu.SMEM)] * 2
        + [pl.BlockSpec(memory_space=pl.ANY)] * len(arrays),
        out_specs=[pl.BlockSpec(memory_space=pltpu.VMEM)] * NX,
        scratch_shapes=[
            pltpu.VMEM((D // PART, PART, 3 * GROUP), jnp.bfloat16),
            pltpu.VMEM((TOKENS, D), jnp.bfloat16),
            pltpu.VMEM((TOKENS, 3 * GROUP), jnp.float32),
            pltpu.VMEM((TOKENS, 3 * GROUP), jnp.bfloat16),
            pltpu.VMEM((TOKENS, TOKENS), jnp.float32),
            pltpu.VMEM((NX, TOKENS // NX, GROUP), jnp.bfloat16),
            pltpu.SemaphoreType.DMA((D // CHUNK, 3)),
            pltpu.SemaphoreType.DMA((8,)),
        ],
        compiler_params=pltpu.CompilerParams(vmem_limit_bytes=44 * 1024 * 1024),
    )(place, span_mask, *arrays)


def per_device(frames_in, qkv_weight, span_mask):
    z, x, y, c = (lax.axis_index(name) for name in AXES)
    group = x // 2
    hold = lax.optimization_barrier

    places = frames_in.reshape(NZ, NX, 8, D)
    places = lax.dynamic_slice(places, (0, 2 * c, 0, 2 * GROUP * y), (NZ, 2, 8, 2 * GROUP))
    low, high = places[..., :GROUP], places[..., GROUP:]
    low = jnp.where(c == 0, low, low[:, ::-1])
    high = jnp.where(c == 0, high[:, ::-1], high)
    packed = jnp.swapaxes(jnp.concatenate([low, high], axis=1), 0, 1).reshape(NZ * NX, 8, GROUP)

    piece = jnp.transpose(qkv_weight, (1, 0, 2))
    first = permute(piece, home)
    other = permute(piece, second)
    slot = jnp.where(c == group, x, 3 - x)
    half = jnp.where(
        slot % 2 == 0,
        jnp.concatenate([first, other], axis=1),
        jnp.concatenate([other, first], axis=1),
    )
    half, packed = hold((half, packed))
    gathered = lax.all_gather(half[None], ("z", "c"), axis=0, tiled=True)
    spread = lax.all_to_all(packed, ("x", "z"), split_axis=0, concat_axis=0, tiled=True)
    spread = jnp.swapaxes(spread.reshape(NX, NZ, 8, GROUP), 0, 1).reshape(TOKENS, GROUP)
    partner = permute(spread, lambda z, x, y, c: (z, 3 - x, y, c))
    pieces = [spread, partner]
    for shift in SHIFTS[1:]:
        for block in (spread, partner):
            pieces.append(permute(block, lambda z, x, y, c, k=shift: (z, x, y - k, c)))

    place = jnp.stack([y, group, slot]).astype(jnp.int32)
    parts = project_and_attend(place, span_mask, gathered, pieces)
    parts = [permute(part, functools.partial(home, k=k)) for k, part in enumerate(parts)]
    parts = [lax.select_n(x, *[parts[k ^ at] for k in range(NX)]) for at in range(NX)]
    output = jnp.stack([part.reshape(NZ, 8, GROUP) for part in parts], axis=1)
    output = lax.all_to_all(output, "z", split_axis=0, concat_axis=0, tiled=True)
    return output.reshape(1, NZ * NX * 8, GROUP)


def solution(mesh):
    fine = Mesh(mesh.devices.reshape(NZ, NX, NY, NC), AXES)
    in_specs = (P(("z", "x"), None, None), P(("z", "x"), None, ("y", "c")), P())
    out_specs = P(("z", "x"), None, ("y", "c"))
    return jax.shard_map(
        per_device, mesh=fine, in_specs=in_specs, out_specs=out_specs, check_vma=False
    )
```
